32 devices in a mesh: dev: 32 (over z, y, x, core).
Axes of the slice: x: 2, y: 2, z: 4, core: 2. Of those that a mesh axis runs over, the one named last changes fastest.
Arguments:
- tokens: bfloat16 [16384, 1280], P('dev'), may hold values from -6 to 6
- lengths: int32 [16], replicated, may hold values from 256 to 1024, as said below
- out_grad: bfloat16 [16384, 1280], P('dev'), may hold values from -6 to 6
- first_gain: bfloat16 [1280], P('dev'), may hold values from 0.5 to 1.5
- first_shift: bfloat16 [1280], P('dev'), may hold values from -3 to 3
- query_weight: bfloat16 [1280, 1280], P('dev'), may hold values from -0.15625 to 0.15625
- query_bias: bfloat16 [1280], P('dev'), may hold values from -3 to 3
- key_weight: bfloat16 [1280, 1280], P('dev'), may hold values from -0.15625 to 0.15625
- value_weight: bfloat16 [1280, 1280], P('dev'), may hold values from -0.15625 to 0.15625
- value_bias: bfloat16 [1280], P('dev'), may hold values from -0.29882812 to 0.29882812
- proj_weight: bfloat16 [1280, 1280], P('dev'), may hold values from -2.5 to 2.5
- proj_bias: bfloat16 [1280], P('dev'), may hold values from -3 to 3
- mid_gain: bfloat16 [1280], P('dev'), may hold values from 0.5 to 1.5
- mid_shift: bfloat16 [1280], P('dev'), may hold values from -3 to 3
- up_weight: bfloat16 [1280, 5120], P('dev'), may hold values from -0.15625 to 0.15625
- up_bias: bfloat16 [5120], P('dev'), may hold values from -3 to 3
- down_weight: bfloat16 [5120, 1280], P('dev'), may hold values from -0.078125 to 0.078125
- down_bias: bfloat16 [1280], P('dev'), may hold values from -3 to 3
Outputs:
- output: bfloat16 [16384, 1280], P('dev')
- input_grad: bfloat16 [16384, 1280], P('dev')
- first_gain_grad: float32 [1280], P('dev')
- first_shift_grad: float32 [1280], P('dev')
- query_weight_grad: float32 [1280, 1280], P('dev')
- query_bias_grad: float32 [1280], P('dev')
- key_weight_grad: float32 [1280, 1280], P('dev')
- value_weight_grad: float32 [1280, 1280], P('dev')
- value_bias_grad: float32 [1280], P('dev')
- proj_weight_grad: float32 [1280, 1280], P('dev')
- proj_bias_grad: float32 [1280], P('dev')
- mid_gain_grad: float32 [1280], P('dev')
- mid_shift_grad: float32 [1280], P('dev')
- up_weight_grad: float32 [1280, 5120], P('dev')
- up_bias_grad: float32 [5120], P('dev')
- down_weight_grad: float32 [5120, 1280], P('dev')
- down_bias_grad: float32 [1280], P('dev')
The draws below stay inside these ranges and needn't reach their ends.
Inputs may be any that keep to these rules, and one draw needn't show every extreme that they name: Clip c holds rows c * 1024 to (c + 1) * 1024 - 1, of which the first lengths[c] are real; in every draw some clip is full.
All inputs are finite; a program needn't handle non-finite values.
Results may differ from the reference program's by a relative error of at most 0.012.
Values may be sent and summed in bfloat16 or wider, within the bound.
No kernel may reach another device: no remote copies, remote signals or barrier semaphores. Data moves between devices by JAX's collectives and lax.ppermute only.
A program may use at most 320 MiB of HBM per device.

```python
from functools import partial
import jax
import jax.numpy as jnp
from jax import lax

D = 1280
H = 16
HD = 80
FF = 5120
CLIP = 1024
CLIPS = 16
TOKENS = 16384


def draw_lengths(key, part):
    key = jax.random.fold_in(key, 11)
    first, second = jax.random.split(key)
    drawn = jax.random.randint(first, (CLIPS,), CLIP // 4, CLIP + 1)
    chosen = jax.random.randint(second, (), 0, CLIPS)
    return jnp.where(jnp.arange(CLIPS) == chosen, CLIP, drawn).astype(jnp.int32)


def steps_of(stream_key, extent, cuts, low, largest):
    def one(axis_at, parts):
        heights = jax.random.uniform(jax.random.fold_in(jax.random.fold_in(stream_key, 6), axis_at), (parts,), jnp.float32, low / len(cuts), largest / len(cuts))
        return jnp.repeat(jnp.exp(heights), extent[axis_at] // parts).reshape((-1,) + (1,) * (len(extent) - axis_at - 1))

    level = one(*cuts[0])
    for cut in cuts[1:]:
        level = level * one(*cut)
    return level


def noise(own_key, shape, width, limit, pieces=(), kind=jnp.bfloat16):
    entries = width * jax.random.normal(own_key, shape, jnp.float32)
    if pieces:
        entries = entries * steps_of(own_key, shape, pieces, -0.22, 0.18)
    return jnp.clip(entries, -limit, limit).astype(kind)


def setup_inputs(seed: int = 0) -> dict:
    key_list = jax.random.split(jax.random.key(seed), 19)
    tokens = noise(key_list[0], (TOKENS, D), 1.0, 6.0, ((0, 32),))
    lengths = draw_lengths(jax.random.fold_in(key_list[18], 71), 0)
    out_grad = noise(key_list[2], (TOKENS, D), 1.0, 6.0, ((0, 32),))
    first_gain = jnp.clip(0.5 + 1.0 * jax.random.uniform(key_list[3], (D,), jnp.float32) ** steps_of(key_list[3], (D,), ((0, 32),), -0.2, 0.2), 0.5, 1.5).astype(jnp.bfloat16)
    first_shift = noise(key_list[4], (D,), 0.5, 3.0, ((0, 32),))
    query_weight = noise(key_list[5], (D, D), D ** -0.5, 0.15625, ((0, 32),))
    query_bias = noise(key_list[6], (D,), 0.5, 3.0, ((0, 32),))
    key_weight = noise(key_list[7], (D, D), D ** -0.5, 0.15625, ((0, 32),))
    value_weight = noise(key_list[8], (D, D), D ** -0.5, 0.15625, ((0, 32),))
    value_bias = noise(key_list[9], (D,), 0.05, 0.29882812, ((0, 32),))
    proj_weight = noise(key_list[10], (D, D), (max(1, D // 256)) ** -0.5, 2.5, ((0, 32),))
    proj_bias = noise(key_list[11], (D,), 0.5, 3.0, ((0, 32),))
    mid_gain = jnp.clip(0.5 + 1.0 * jax.random.uniform(key_list[12], (D,), jnp.float32) ** steps_of(key_list[12], (D,), ((0, 32),), -0.2, 0.2), 0.5, 1.5).astype(jnp.bfloat16)
    mid_shift = noise(key_list[13], (D,), 0.5, 3.0, ((0, 32),))
    up_weight = noise(key_list[14], (D, FF), D ** -0.5, 0.15625, ((0, 32),))
    up_bias = noise(key_list[15], (FF,), 0.5, 3.0, ((0, 32),))
    down_weight = noise(key_list[16], (FF, D), FF ** -0.5, 0.078125, ((0, 32),))
    down_bias = noise(key_list[17], (D,), 0.5, 3.0, ((0, 32),))
    return dict(tokens=tokens, lengths=lengths, out_grad=out_grad, first_gain=first_gain, first_shift=first_shift, query_weight=query_weight, query_bias=query_bias, key_weight=key_weight, value_weight=value_weight, value_bias=value_bias, proj_weight=proj_weight, proj_bias=proj_bias, mid_gain=mid_gain, mid_shift=mid_shift, up_weight=up_weight, up_bias=up_bias, down_weight=down_weight, down_bias=down_bias)


@jax.custom_vjp
def low(v):
    return lax.optimization_barrier(v.astype(jnp.bfloat16)).astype(jnp.float32)

@jax.custom_vjp
def low_back(v):
    return v

def low_keep(v):
    return (low(v), None)

def low_pass(kept, grad):
    return (grad,)

def back_keep(v):
    return (v, None)

def back_low(kept, grad):
    return (low(grad),)
low.defvjp(low_keep, low_pass)
low_back.defvjp(back_keep, back_low)
EPS = 1e-05
NEG = -1e+30

def layer_norm(values, gain, shift):
    center = values - lax.optimization_barrier(jnp.mean(values, axis=-1, keepdims=True))
    spread = lax.optimization_barrier(jnp.mean(center * center, axis=-1, keepdims=True))
    return center * lax.rsqrt(spread + EPS) * gain + shift

def matmul(left, right):
    return jnp.dot(left, right, precision=lax.Precision.HIGHEST)

def attend(q_clip, k_clip, v_clip, length):
    scale = HD ** (-0.5)
    scores = jnp.einsum('qhd,khd->hqk', q_clip, k_clip, precision=lax.Precision.HIGHEST) * scale
    scores = low_back(scores)
    live_keys = jnp.arange(CLIP) < length
    scores = jnp.where(live_keys[None, None, :], scores, NEG)
    top = lax.optimization_barrier(jnp.max(scores, axis=-1, keepdims=True))
    weights = jnp.exp(scores - top)
    probs = weights / lax.optimization_barrier(jnp.sum(weights, axis=-1, keepdims=True))
    return jnp.einsum('hqk,khd->qhd', low(probs), v_clip, precision=lax.Precision.HIGHEST)

def forward(lengths, inputs, pre_gain, pre_shift, w_query, b_query, w_key, w_value, b_value, w_proj, b_proj, mid_gain, mid_shift, w_up, b_up, w_down, b_down):
    normed = low(layer_norm(inputs, pre_gain, pre_shift))
    queries = low(low_back(matmul(normed, low(w_query)) + b_query))
    keys = low(low_back(matmul(normed, low(w_key))))
    values = low(low_back(matmul(normed, low(w_value)) + b_value))
    shape = (CLIPS, CLIP, H, HD)
    clip_fn = jax.checkpoint(attend)

    def one_clip(carry, operands):
        return (carry, clip_fn(*operands))
    carry, attended = lax.scan(one_clip, None, (queries.reshape(shape), keys.reshape(shape), values.reshape(shape), lengths))
    attended = low(low_back(attended.reshape(TOKENS, D)))
    branch = low_back(matmul(attended, low(w_proj)) + b_proj)
    mid = inputs + branch
    mid_normed = low(layer_norm(mid, mid_gain, mid_shift))
    pre_act = low_back(matmul(mid_normed, low(w_up)) + b_up)
    activ = low(jax.nn.gelu(pre_act, approximate=False))
    return mid + matmul(activ, low(w_down)) + b_down

def reference(tokens, lengths, out_grad, first_gain, first_shift, query_weight, query_bias, key_weight, value_weight, value_bias, proj_weight, proj_bias, mid_gain, mid_shift, up_weight, up_bias, down_weight, down_bias):
    params = tuple((item.astype(jnp.float32) for item in (first_gain, first_shift, query_weight, query_bias, key_weight, value_weight, value_bias, proj_weight, proj_bias, mid_gain, mid_shift, up_weight, up_bias, down_weight, down_bias)))
    inputs = tokens.astype(jnp.float32)
    row_ids = jnp.arange(TOKENS).astype(jnp.int32)
    live = row_ids % CLIP < lengths[row_ids // CLIP]
    grad = jnp.where(live[:, None], out_grad.astype(jnp.float32), 0.0)
    result, pull = jax.vjp(partial(forward, lengths), inputs, *params)
    grads = pull(grad)
    return (result.astype(jnp.bfloat16), grads[0].astype(jnp.bfloat16), grads[1], grads[2], grads[3], grads[4], grads[5], grads[6], grads[7], grads[8], grads[9], grads[10], grads[11], grads[12], grads[13], grads[14], grads[15])
```

```python
import functools
import math

import jax
import jax.numpy as jnp
from jax import lax
from jax.experimental import pallas as pl
from jax.experimental.pallas import tpu as pltpu
from jax.sharding import PartitionSpec as P

HD = 80
EPS = 1e-05
NEG = -1e30
SCALE = HD**-0.5
LOG2E = math.log2(math.e)
BF = jnp.bfloat16
F32 = jnp.float32
VECTORS = 128


def contract(left, right, left_dim, right_dim):
    return lax.dot_general(
        left, right, (((left_dim,), (right_dim,)), ((), ())), preferred_element_type=F32
    )


def attend_kernel(length, qkv, attended, log_total):
    rows = qkv.shape[2]
    keys = qkv[1].T
    dead = lax.broadcasted_iota(jnp.int32, (rows, 1), 0) >= length[0]
    scores = contract(keys, qkv[0], 1, 0) + jnp.where(dead, NEG, 0.0).astype(F32)
    top = jnp.max(scores, axis=0, keepdims=True)
    weights = jnp.exp2((scores - top) * (SCALE * LOG2E))
    total = jnp.sum(weights, axis=0, keepdims=True)
    probs = (weights * (1.0 / total)).astype(BF)
    attended[...] = contract(qkv[2], probs, 1, 0).astype(BF)
    log_total[0] = top * (SCALE * LOG2E) + jnp.log2(total)


def attend(length, qkv):
    _, width, rows = qkv.shape
    heads = width // HD
    return pl.pallas_call(
        attend_kernel,
        grid=(heads,),
        in_specs=[
            pl.BlockSpec(memory_space=pltpu.SMEM),
            pl.BlockSpec((3, HD, rows), lambda h: (0, h, 0)),
        ],
        out_specs=[
            pl.BlockSpec((HD, rows), lambda h: (h, 0)),
            pl.BlockSpec((1, 1, rows), lambda h: (h, 0, 0)),
        ],
        out_shape=[
            jax.ShapeDtypeStruct((width, rows), BF),
            jax.ShapeDtypeStruct((heads, 1, rows), F32),
        ],
        compiler_params=pltpu.CompilerParams(vmem_limit_bytes=40 << 20),
        cost_estimate=pl.CostEstimate(
            flops=12 * width * rows * rows,
            bytes_accessed=8 * width * rows,
            transcendentals=heads * rows * rows,
        ),
    )(length, qkv)


def attend_back_kernel(length, qkv, out_grad, log_total, grads, key_sum, value_sum, *, step):
    rows = qkv.shape[2]
    keys = qkv[1].T
    values = qkv[2].T
    dead = lax.broadcasted_iota(jnp.int32, (rows, 1), 0) >= length[0]
    bias = jnp.where(dead, NEG, 0.0).astype(F32)
    for at in range(0, rows, step):
        part = slice(at, at + step)
        queries = qkv[0, :, part]
        out_part = out_grad[:, part]
        scores = contract(keys, queries, 1, 0) + bias
        probs = jnp.exp2(scores * (SCALE * LOG2E) - log_total[0, :, part])
        prob_grad = contract(values, out_part, 1, 0)
        inner = jnp.sum(probs * prob_grad, axis=0, keepdims=True)
        score_grad = (probs * (prob_grad - inner)).astype(BF)
        probs_low = probs.astype(BF)
        grads[0, :, part] = (contract(qkv[1], score_grad, 1, 0) * SCALE).astype(BF)
        key_part = contract(queries, score_grad, 1, 1)
        value_part = contract(out_part, probs_low, 1, 1)
        if at == 0:
            key_sum[...] = key_part
            value_sum[...] = value_part
        else:
            key_sum[...] += key_part
            value_sum[...] += value_part
    grads[1] = (key_sum[...] * SCALE).astype(BF)
    grads[2] = value_sum[...].astype(BF)


def attend_back(length, qkv, out_grad, log_total):
    _, width, rows = qkv.shape
    heads = width // HD
    return pl.pallas_call(
        functools.partial(attend_back_kernel, step=min(512, rows)),
        grid=(heads,),
        in_specs=[
            pl.BlockSpec(memory_space=pltpu.SMEM),
            pl.BlockSpec((3, HD, rows), lambda h: (0, h, 0)),
            pl.BlockSpec((HD, rows), lambda h: (h, 0)),
            pl.BlockSpec((1, 1, rows), lambda h: (h, 0, 0)),
        ],
        out_specs=pl.BlockSpec((3, HD, rows), lambda h: (0, h, 0)),
        out_shape=jax.ShapeDtypeStruct((3, width, rows), BF),
        scratch_shapes=[pltpu.VMEM((HD, rows), F32), pltpu.VMEM((HD, rows), F32)],
        compiler_params=pltpu.CompilerParams(vmem_limit_bytes=48 << 20),
        cost_estimate=pl.CostEstimate(
            flops=22 * width * rows * rows,
            bytes_accessed=14 * width * rows,
            transcendentals=heads * rows * rows,
        ),
    )(length, qkv, out_grad, log_total)


def make_body(devices):
    chips = devices // 2
    lines = chips // 4

    def place(line, b, a, core):
        return ((line * 2 + b) * 2 + a) * 2 + core

    every = [
        (line, b, a, core)
        for line in range(lines)
        for b in range(2)
        for a in range(2)
        for core in range(2)
    ]
    core_pairs = [(place(*at), place(at[0], at[1], at[2], 1 - at[3])) for at in every]
    a_pairs = [(place(*at), place(at[0], at[1], 1 - at[2], at[3])) for at in every]
    b_pairs = [(place(*at), place(at[0], 1 - at[1], at[2], at[3])) for at in every]
    groups = [
        [place(line, b, a, core) for line in range(lines)]
        for b in range(2)
        for a in range(2)
        for core in range(2)
    ]
    half = lines // 2

    def swap_core(value):
        return lax.ppermute(value, "dev", core_pairs)

    def swap_a(value):
        return lax.ppermute(value, "dev", a_pairs)

    def swap_b(value):
        return lax.ppermute(value, "dev", b_pairs)

    def body(
        tokens,
        lengths,
        out_grad,
        first_gain,
        first_shift,
        query_weight,
        query_bias,
        key_weight,
        value_weight,
        value_bias,
        proj_weight,
        proj_bias,
        mid_gain,
        mid_shift,
        up_weight,
        up_bias,
        down_weight,
        down_bias,
    ):
        position = lax.axis_index("dev")
        core = position % 2
        chip = position // 2
        at_a = chip % 2
        at_b = (chip // 2) % 2
        own_rows, width = tokens.shape
        rows = 2 * own_rows
        shard = query_weight.shape[0]
        side = width // 2
        hidden = up_weight.shape[1]
        block = hidden // devices
        spread = block // shard
        length = lax.dynamic_slice(lengths, (chip,), (1,))

        def both(own, other):
            first = jnp.where(core == 0, own, other)
            second = jnp.where(core == 0, other, own)
            return jnp.concatenate([first, second], axis=0)

        def columns(weight, which):
            return lax.dynamic_slice(weight, (0, which * side), (weight.shape[0], side))

        def blocks(weight, which):
            cut = weight.reshape(weight.shape[0], chips, 2, block)
            return lax.dynamic_index_in_dim(cut, which, 2, keepdims=False).reshape(
                weight.shape[0], chips * block
            )

        def gather(value):
            line = lax.all_gather(value, "dev", axis=0, axis_index_groups=groups)
            from_a = swap_a(line)
            from_b = swap_b(line)
            far_low = swap_a(from_b[:half])
            far_high = swap_b(from_a[half:])
            whole = jnp.zeros((lines, 2, 2) + value.shape, value.dtype)
            zero = jnp.int32(0)

            def put(whole, part, line_at, b, a):
                return lax.dynamic_update_slice(
                    whole, part[:, None, None], (jnp.int32(line_at), b, a, zero, zero)
                )

            whole = put(whole, line, 0, at_b, at_a)
            whole = put(whole, from_a, 0, at_b, 1 - at_a)
            whole = put(whole, from_b, 0, 1 - at_b, at_a)
            whole = put(whole, far_low, 0, 1 - at_b, 1 - at_a)
            whole = put(whole, far_high, half, 1 - at_b, 1 - at_a)
            return whole.reshape(chips * value.shape[0], value.shape[1])

        def scatter_plane(whole):
            parts = whole.reshape(lines, 2, 2, whole.shape[0] // chips, whole.shape[1])

            def pick(b, a):
                at = lax.dynamic_index_in_dim(parts, b, 1, keepdims=False)
                return lax.dynamic_index_in_dim(at, a, 1, keepdims=False)

            far = pick(1 - at_b, 1 - at_a).astype(BF)
            far_low = swap_a(far[:half])
            far_high = swap_b(far[half:])
            to_a = pick(at_b, 1 - at_a).astype(F32)
            to_b = pick(1 - at_b, at_a).astype(F32)
            to_a = jnp.concatenate([to_a[:half], to_a[half:] + far_high.astype(F32)], axis=0)
            to_b = jnp.concatenate([to_b[:half] + far_low.astype(F32), to_b[half:]], axis=0)
            from_a = swap_a(to_a.astype(BF))
            from_b = swap_b(to_b.astype(BF))
            own = pick(at_b, at_a).astype(F32) + from_a.astype(F32) + from_b.astype(F32)
            return own.astype(BF)

        def scatter_line(parts):
            return lax.psum_scatter(
                parts, "dev", scatter_dimension=0, axis_index_groups=groups
            )

        other = 1 - core
        vectors = jnp.stack(
            [first_gain, first_shift, query_bias, value_bias, proj_bias, mid_gain, mid_shift, down_bias],
            axis=1,
        )
        vectors = jnp.concatenate([vectors, up_bias.reshape(shard, spread)], axis=1)
        vectors = jnp.pad(vectors, ((0, 0), (0, VECTORS - vectors.shape[1])))
        own_qkv = jnp.concatenate(
            [columns(query_weight, core), columns(key_weight, core), columns(value_weight, core), vectors], axis=1
        )
        give_qkv = jnp.concatenate(
            [columns(query_weight, other), columns(key_weight, other), columns(value_weight, other), vectors], axis=1
        )
        qkv_shard = both(own_qkv, swap_core(give_qkv))
        all_tokens = both(tokens, swap_core(tokens)).astype(F32)
        rest_own = jnp.concatenate([columns(proj_weight, core), blocks(up_weight, core)], axis=1)
        rest_give = jnp.concatenate([columns(proj_weight, other), blocks(up_weight, other)], axis=1)
        rest_shard = both(rest_own, swap_core(rest_give))
        all_grad = both(out_grad, swap_core(out_grad))
        live = jnp.arange(rows) < length[0]
        grad_low = jnp.where(live[:, None], all_grad, jnp.zeros_like(all_grad))

        w_qkv_wide = gather(qkv_shard)
        w_proj_side = gather(rest_shard[:, :side])
        w_up = gather(rest_shard[:, side:])
        w_down = gather(down_weight)

        w_qkv = w_qkv_wide[:, : 3 * side]
        table = w_qkv_wide[:, 3 * side :].astype(F32).T
        gain_one, shift_one, b_query, b_value, b_proj, gain_two, shift_two, b_down = (
            table[i] for i in range(8)
        )
        hidden_bias = table[8 : 8 + spread].reshape(spread, chips, 2, shard)
        hidden_bias = lax.dynamic_index_in_dim(hidden_bias, core, 2, keepdims=False)
        hidden_bias = hidden_bias.transpose(1, 2, 0).reshape(chips * block)
        w_proj_other = swap_core(w_proj_side)
        w_proj = jnp.concatenate(
            [
                jnp.where(core == 0, w_proj_side, w_proj_other),
                jnp.where(core == 0, w_proj_other, w_proj_side),
            ],
            axis=1,
        )

        def own_side(vector):
            return lax.dynamic_slice(vector, (core * side,), (side,))

        def normalize(value, gain, shift):
            center = value - jnp.mean(value, axis=-1, keepdims=True)
            spread_of = jnp.mean(center * center, axis=-1, keepdims=True)
            scale = lax.rsqrt(spread_of + EPS)
            hat = center * scale
            return hat * gain + shift, hat, scale

        def normalize_back(grad, hat, scale, gain):
            scaled = grad * gain
            mean = jnp.mean(scaled, axis=-1, keepdims=True)
            dot = jnp.mean(scaled * hat, axis=-1, keepdims=True)
            return (
                (scaled - mean - hat * dot) * scale,
                jnp.sum(grad * hat, axis=0),
                jnp.sum(grad, axis=0),
            )

        normed = normalize(all_tokens, gain_one, shift_one)[0].astype(BF)
        qkv_bias = jnp.concatenate([own_side(b_query), jnp.zeros((side,), F32), own_side(b_value)])
        qkv = (contract(w_qkv, normed, 0, 1) + qkv_bias[:, None]).astype(BF).reshape(3, side, rows)
        attended_own, log_total = attend(length, qkv)
        attended = both(attended_own, swap_core(attended_own))
        mid = all_tokens + contract(attended, w_proj, 0, 0) + b_proj
        mid_normed, mid_hat, mid_scale = normalize(mid, gain_two, shift_two)
        mid_low = mid_normed.astype(BF)
        pre_act = contract(mid_low, w_up, 1, 0) + hidden_bias
        below = 0.5 + 0.5 * lax.erf(pre_act * math.sqrt(0.5))
        activ = (pre_act * below).astype(BF)
        slope = (below + pre_act * (jnp.exp(-0.5 * pre_act * pre_act) * (1.0 / math.sqrt(2.0 * math.pi)))).astype(BF)
        down_grad = contract(activ, grad_low, 0, 0).astype(BF)
        down_part = contract(activ, w_down, 1, 0)

        def rows_of(value, which):
            return lax.dynamic_slice(value, (which * own_rows, 0), (own_rows, value.shape[1]))

        down_other = swap_core(rows_of(down_part, other).astype(BF))
        output = (
            rows_of(mid, core) + rows_of(down_part, core) + down_other.astype(F32) + b_down
        ).astype(BF)

        grad_full = grad_low.astype(F32)
        down_b_grad = 0.5 * jnp.sum(grad_full, axis=0)
        pre_grad = (contract(grad_low, w_down, 1, 1) * slope.astype(F32)).astype(BF)
        up_grad = contract(mid_low, pre_grad, 0, 0).astype(BF)
        up_b_grad = jnp.sum(pre_grad.astype(F32), axis=0)
        mid_part = contract(pre_grad, w_up, 1, 1)
        mid_e = mid_part + swap_core(mid_part.astype(BF)).astype(F32)
        mid_back, gain_two_grad, shift_two_grad = normalize_back(mid_e, mid_hat, mid_scale, gain_two)
        mid_grad = grad_full + mid_back
        branch = mid_grad.astype(BF)
        branch_side = lax.dynamic_slice(branch, (0, core * side), (rows, side))
        proj_grad = contract(attended, branch_side, 1, 0).astype(BF)
        proj_b_grad = 0.5 * jnp.sum(branch.astype(F32), axis=0)
        w_proj_heads = lax.dynamic_slice(w_proj, (core * side, 0), (side, width))
        attended_grad = contract(w_proj_heads, branch, 1, 1).astype(BF)
        qkv_back = attend_back(length, qkv, attended_grad, log_total).reshape(3 * side, rows)
        qkv_grad = contract(normed, qkv_back, 0, 1).astype(BF)
        qkv_b_grad = jnp.sum(qkv_back.astype(F32), axis=1)
        normed_part = contract(qkv_back, w_qkv, 0, 1)
        normed_other = swap_core(rows_of(normed_part, other).astype(BF))
        normed_e = rows_of(normed_part, core) + normed_other.astype(F32)
        _, first_hat, first_scale = normalize(tokens.astype(F32), gain_one, shift_one)
        first_back, gain_one_grad, shift_one_grad = normalize_back(normed_e, first_hat, first_scale, gain_one)
        input_grad = (rows_of(mid_grad, core) + first_back).astype(BF)

        def on_side(vector):
            return lax.dynamic_update_slice(jnp.zeros((width,), F32), vector, (core * side,))

        up_rows = up_b_grad.reshape(chips, 1, shard, spread)
        up_rows = lax.dynamic_update_slice(
            jnp.zeros((chips, 2, shard, spread), F32), up_rows, (0, core, 0, 0)
        ).reshape(width, spread)
        sums = jnp.stack(
            [
                gain_one_grad,
                shift_one_grad,
                on_side(qkv_b_grad[:side]),
                on_side(qkv_b_grad[2 * side :]),
                proj_b_grad,
                0.5 * gain_two_grad,
                0.5 * shift_two_grad,
                down_b_grad,
            ],
            axis=1,
        )
        sums = jnp.concatenate([sums, up_rows], axis=1)
        sums = jnp.pad(sums, ((0, 0), (0, VECTORS - sums.shape[1])))

        down_sum = scatter_line(scatter_plane(down_grad))
        up_sum = scatter_line(scatter_plane(up_grad))
        proj_sum = scatter_line(scatter_plane(proj_grad))
        qkv_sum = scatter_line(scatter_plane(qkv_grad))
        vector_sum = scatter_line(scatter_plane(sums))

        def finish(sum_of, which):
            return lax.dynamic_slice(sum_of, (which * shard, 0), (shard, sum_of.shape[1]))

        tail = jnp.concatenate([proj_sum, qkv_sum, vector_sum, up_sum], axis=1)
        mine = finish(tail, core)
        theirs = swap_core(finish(tail, other))
        left = jnp.where(core == 0, mine, theirs).astype(F32)
        right = jnp.where(core == 0, theirs, mine).astype(F32)

        def joined(start):
            return jnp.concatenate([left[:, start : start + side], right[:, start : start + side]], axis=1)

        at_vectors = 4 * side
        vector_rows = (
            left[:, at_vectors : at_vectors + 8 + spread] + right[:, at_vectors : at_vectors + 8 + spread]
        )
        at_up = at_vectors + VECTORS
        up_all = jnp.stack(
            [
                left[:, at_up:].reshape(shard, chips, block),
                right[:, at_up:].reshape(shard, chips, block),
            ],
            axis=2,
        ).reshape(shard, hidden)
        return (
            output,
            input_grad,
            vector_rows[:, 0],
            vector_rows[:, 1],
            joined(side),
            vector_rows[:, 2],
            joined(2 * side),
            joined(3 * side),
            vector_rows[:, 3],
            joined(0),
            vector_rows[:, 4],
            vector_rows[:, 5],
            vector_rows[:, 6],
            up_all,
            vector_rows[:, 8 : 8 + spread].reshape(block),
            down_sum.astype(F32),
            vector_rows[:, 7],
        )

    return body


def solution(mesh):
    matrix, vector = P("dev", None), P("dev")
    return jax.shard_map(
        make_body(mesh.shape["dev"]),
        mesh=mesh,
        in_specs=(
            matrix,
            P(),
            matrix,
            vector,
            vector,
            matrix,
            vector,
            matrix,
            matrix,
            vector,
            matrix,
            vector,
            vector,
            vector,
            matrix,
            vector,
            matrix,
            vector,
        ),
        out_specs=(
            matrix,
            matrix,
            vector,
            vector,
            matrix,
            vector,
            matrix,
            matrix,
            vector,
            matrix,
            vector,
            vector,
            vector,
            matrix,
            vector,
            matrix,
            vector,
        ),
        check_vma=False,
    )
```

```python
import functools
import math

import jax
import jax.numpy as jnp
from jax import lax
from jax.experimental import pallas as pl
from jax.experimental.pallas import tpu as pltpu
from jax.sharding import PartitionSpec as P

HD = 80
EPS = 1e-05
NEG = -1e30
SCALE = HD**-0.5
LOG2E = math.log2(math.e)
BF = jnp.bfloat16
F32 = jnp.float32
VECTORS = 128
SMALL = pl.CostEstimate(flops=1, bytes_accessed=1, transcendentals=0)


def contract(left, right, left_dim, right_dim):
    return lax.dot_general(
        left, right, (((left_dim,), (right_dim,)), ((), ())), preferred_element_type=F32
    )


def attend_kernel(length, qkv, attended, log_total):
    rows = qkv.shape[2]
    keys = qkv[1].T
    dead = lax.broadcasted_iota(jnp.int32, (rows, 1), 0) >= length[0]
    scores = contract(keys, qkv[0], 1, 0) + jnp.where(dead, NEG, 0.0).astype(F32)
    top = jnp.max(scores, axis=0, keepdims=True)
    weights = jnp.exp2((scores - top) * (SCALE * LOG2E))
    total = jnp.sum(weights, axis=0, keepdims=True)
    probs = (weights * (1.0 / total)).astype(BF)
    attended[...] = contract(qkv[2], probs, 1, 0).astype(BF)
    log_total[0] = top * (SCALE * LOG2E) + jnp.log2(total)


def attend(length, qkv):
    _, width, rows = qkv.shape
    heads = width // HD
    return pl.pallas_call(
        attend_kernel,
        grid=(heads,),
        in_specs=[
            pl.BlockSpec(memory_space=pltpu.SMEM),
            pl.BlockSpec((3, HD, rows), lambda h: (0, h, 0)),
        ],
        out_specs=[
            pl.BlockSpec((HD, rows), lambda h: (h, 0)),
            pl.BlockSpec((1, 1, rows), lambda h: (h, 0, 0)),
        ],
        out_shape=[
            jax.ShapeDtypeStruct((width, rows), BF),
            jax.ShapeDtypeStruct((heads, 1, rows), F32),
        ],
        compiler_params=pltpu.CompilerParams(vmem_limit_bytes=40 << 20),
        cost_estimate=SMALL,
    )(length, qkv)


def attend_back_kernel(length, qkv, out_grad, log_total, grads, key_sum, value_sum, *, step):
    rows = qkv.shape[2]
    keys = qkv[1].T
    values = qkv[2].T
    dead = lax.broadcasted_iota(jnp.int32, (rows, 1), 0) >= length[0]
    bias = jnp.where(dead, NEG, 0.0).astype(F32)
    for at in range(0, rows, step):
        part = slice(at, at + step)
        queries = qkv[0, :, part]
        out_part = out_grad[:, part]
        scores = contract(keys, queries, 1, 0) + bias
        probs = jnp.exp2(scores * (SCALE * LOG2E) - log_total[0, :, part])
        prob_grad = contract(values, out_part, 1, 0)
        inner = jnp.sum(probs * prob_grad, axis=0, keepdims=True)
        score_grad = (probs * (prob_grad - inner)).astype(BF)
        probs_low = probs.astype(BF)
        grads[0, :, part] = (contract(qkv[1], score_grad, 1, 0) * SCALE).astype(BF)
        key_part = contract(queries, score_grad, 1, 1)
        value_part = contract(out_part, probs_low, 1, 1)
        if at == 0:
            key_sum[...] = key_part
            value_sum[...] = value_part
        else:
            key_sum[...] += key_part
            value_sum[...] += value_part
    grads[1] = (key_sum[...] * SCALE).astype(BF)
    grads[2] = value_sum[...].astype(BF)


def attend_back(length, qkv, out_grad, log_total):
    _, width, rows = qkv.shape
    heads = width // HD
    return pl.pallas_call(
        functools.partial(attend_back_kernel, step=min(512, rows)),
        grid=(heads,),
        in_specs=[
            pl.BlockSpec(memory_space=pltpu.SMEM),
            pl.BlockSpec((3, HD, rows), lambda h: (0, h, 0)),
            pl.BlockSpec((HD, rows), lambda h: (h, 0)),
            pl.BlockSpec((1, 1, rows), lambda h: (h, 0, 0)),
        ],
        out_specs=pl.BlockSpec((3, HD, rows), lambda h: (0, h, 0)),
        out_shape=jax.ShapeDtypeStruct((3, width, rows), BF),
        scratch_shapes=[pltpu.VMEM((HD, rows), F32), pltpu.VMEM((HD, rows), F32)],
        compiler_params=pltpu.CompilerParams(vmem_limit_bytes=48 << 20),
        cost_estimate=SMALL,
    )(length, qkv, out_grad, log_total)


def product_kernel(left, right, out):
    out[...] = contract(left[...], right[...], 1, 0).astype(BF)


def product(left, right):
    rows, depth = left.shape
    width = right.shape[1]
    return pl.pallas_call(
        product_kernel,
        grid=(width // 256,),
        in_specs=[
            pl.BlockSpec((rows, depth), lambda i: (0, 0), pipeline_mode=pl.Buffered(1)),
            pl.BlockSpec((depth, 256), lambda i: (0, i)),
        ],
        out_specs=pl.BlockSpec((rows, 256), lambda i: (0, i)),
        out_shape=jax.ShapeDtypeStruct((rows, width), BF),
        compiler_params=pltpu.CompilerParams(vmem_limit_bytes=16 << 20),
        cost_estimate=SMALL,
    )(left, right)


def norm_back_kernel(
    core, mid, part, other, grad, gain, heads, attended,
    mid_grad, attended_grad, proj_grad, gain_sum, shift_sum, branch_sum, total, held,
):
    at = pl.program_id(0)
    value = mid[...]
    center = value - jnp.mean(value, axis=-1, keepdims=True)
    scale = lax.rsqrt(jnp.mean(center * center, axis=-1, keepdims=True) + EPS)
    hat = center * scale
    error = part[...].astype(F32) + other[...].astype(F32)
    scaled = error * gain[...]
    mean = jnp.mean(scaled, axis=-1, keepdims=True)
    dot = jnp.mean(scaled * hat, axis=-1, keepdims=True)
    summed = grad[...].astype(F32) + (scaled - mean - hat * dot) * scale
    low = summed.astype(BF)
    mid_grad[...] = summed
    held[...] = low
    attended_grad[...] = contract(heads[...], low, 1, 1).astype(BF)
    side = proj_grad.shape[1]
    columns = held[:, pl.ds(pl.multiple_of(core[0] * side, 128), side)]

    @pl.when(at == 0)
    def _():
        total[...] = jnp.zeros_like(total)
        gain_sum[...] = jnp.zeros_like(gain_sum)
        shift_sum[...] = jnp.zeros_like(shift_sum)
        branch_sum[...] = jnp.zeros_like(branch_sum)

    total[...] += contract(attended[...], columns, 1, 0)
    gain_sum[...] += jnp.sum(error * hat, axis=0, keepdims=True)
    shift_sum[...] += jnp.sum(error, axis=0, keepdims=True)
    branch_sum[...] += jnp.sum(low.astype(F32), axis=0, keepdims=True)

    @pl.when(at == pl.num_programs(0) - 1)
    def _():
        proj_grad[...] = total[...].astype(BF)


def norm_back(core, mid, part, other, grad, gain, weight, attended):
    rows, width = mid.shape
    side = width // 2
    cut = 256
    row = pl.BlockSpec((cut, width), lambda i, core: (i, 0))
    one = pl.BlockSpec((1, width), lambda i, core: (0, 0))
    return pl.pallas_call(
        norm_back_kernel,
        grid_spec=pltpu.PrefetchScalarGridSpec(
            num_scalar_prefetch=1,
            grid=(rows // cut,),
            in_specs=[
                row,
                row,
                row,
                row,
                one,
                pl.BlockSpec((side, width), lambda i, core: (core[0], 0)),
                pl.BlockSpec((width, cut), lambda i, core: (0, i)),
            ],
            out_specs=[
                row,
                pl.BlockSpec((side, cut), lambda i, core: (0, i)),
                pl.BlockSpec((width, side), lambda i, core: (0, 0)),
                one,
                one,
                one,
            ],
            scratch_shapes=[pltpu.VMEM((width, side), F32), pltpu.VMEM((cut, width), BF)],
        ),
        out_shape=[
            jax.ShapeDtypeStruct((rows, width), F32),
            jax.ShapeDtypeStruct((side, rows), BF),
            jax.ShapeDtypeStruct((width, side), BF),
            jax.ShapeDtypeStruct((1, width), F32),
            jax.ShapeDtypeStruct((1, width), F32),
            jax.ShapeDtypeStruct((1, width), F32),
        ],
        compiler_params=pltpu.CompilerParams(vmem_limit_bytes=28 << 20),
        cost_estimate=SMALL,
    )(core, mid, part, other, grad, gain.reshape(1, width), weight, attended)


def first_back_kernel(core, tokens, part, other, mid_grad, gain, grad, gain_sum, shift_sum):
    value = tokens[...].astype(F32)
    center = value - jnp.mean(value, axis=-1, keepdims=True)
    scale = lax.rsqrt(jnp.mean(center * center, axis=-1, keepdims=True) + EPS)
    hat = center * scale
    error = part[...].astype(F32) + other[...].astype(F32)
    scaled = error * gain[...]
    mean = jnp.mean(scaled, axis=-1, keepdims=True)
    dot = jnp.mean(scaled * hat, axis=-1, keepdims=True)
    grad[...] = (mid_grad[...] + (scaled - mean - hat * dot) * scale).astype(BF)

    @pl.when(pl.program_id(0) == 0)
    def _():
        gain_sum[...] = jnp.zeros_like(gain_sum)
        shift_sum[...] = jnp.zeros_like(shift_sum)

    gain_sum[...] += jnp.sum(error * hat, axis=0, keepdims=True)
    shift_sum[...] += jnp.sum(error, axis=0, keepdims=True)


def first_back(core, tokens, part, other, mid_grad, gain):
    rows, width = tokens.shape
    cut = 256
    steps = rows // cut
    own = pl.BlockSpec((cut, width), lambda i, core: (i, 0))
    mine = pl.BlockSpec((cut, width), lambda i, core: (core[0] * steps + i, 0))
    one = pl.BlockSpec((1, width), lambda i, core: (0, 0))
    return pl.pallas_call(
        first_back_kernel,
        grid_spec=pltpu.PrefetchScalarGridSpec(
            num_scalar_prefetch=1,
            grid=(steps,),
            in_specs=[own, mine, own, mine, one],
            out_specs=[own, one, one],
        ),
        out_shape=[
            jax.ShapeDtypeStruct((rows, width), BF),
            jax.ShapeDtypeStruct((1, width), F32),
            jax.ShapeDtypeStruct((1, width), F32),
        ],
        compiler_params=pltpu.CompilerParams(vmem_limit_bytes=20 << 20),
        cost_estimate=SMALL,
    )(core, tokens, part, other, mid_grad, gain.reshape(1, width))


def join_kernel(plane, line, from_a, from_b, far_low, far_high, *wholes):
    turn, at = pl.program_id(0), pl.program_id(1)
    half = pl.num_programs(1) // 2

    def put(source):
        start = 0
        for whole in wholes:
            stop = start + whole.shape[-1]
            whole[0, 0, 0] = source[0, :, start:stop]
            start = stop

    pl.when(turn == 0)(lambda: put(line))
    pl.when(turn == 1)(lambda: put(from_a))
    pl.when(turn == 2)(lambda: put(from_b))
    pl.when((turn == 3) & (at < half))(lambda: put(far_low))
    pl.when((turn == 3) & (at >= half))(lambda: put(far_high))


def join(plane, line, near, far, cuts):
    lines, shard, width = line.shape
    half = lines // 2

    def source(turn_of):
        def at(turn, i, plane):
            return (jnp.where(turn == turn_of, i, jnp.where(turn < turn_of, 0, lines - 1)), 0, 0)

        return pl.BlockSpec((1, shard, width), at)

    def low(turn, i, plane):
        return (jnp.where(turn == 3, jnp.minimum(i, half - 1), 0), 0, 0)

    def high(turn, i, plane):
        return (jnp.where(turn == 3, jnp.maximum(i - half, 0), 0), 0, 0)

    def target(turn, i, plane):
        a, b = plane[0], plane[1]
        return (i, jnp.where(turn >= 2, 1 - b, b), jnp.where(turn % 2 == 1, 1 - a, a), 0, 0)

    wholes = pl.pallas_call(
        join_kernel,
        grid_spec=pltpu.PrefetchScalarGridSpec(
            num_scalar_prefetch=1,
            grid=(4, lines),
            in_specs=[
                source(0),
                source(1),
                source(2),
                pl.BlockSpec((1, shard, width), low),
                pl.BlockSpec((1, shard, width), high),
            ],
            out_specs=[pl.BlockSpec((1, 1, 1, shard, cut), target) for cut in cuts],
        ),
        out_shape=[jax.ShapeDtypeStruct((lines, 2, 2, shard, cut), line.dtype) for cut in cuts],
        compiler_params=pltpu.CompilerParams(vmem_limit_bytes=24 << 20),
        cost_estimate=SMALL,
    )(plane, line, *near, *far)
    return [whole.reshape(lines * 4 * shard, whole.shape[-1]) for whole in wholes]


def make_body(devices):
    chips = devices // 2
    lines = chips // 4

    def place(line, b, a, core):
        return ((line * 2 + b) * 2 + a) * 2 + core

    every = [
        (line, b, a, core)
        for line in range(lines)
        for b in range(2)
        for a in range(2)
        for core in range(2)
    ]
    core_pairs = [(place(*at), place(at[0], at[1], at[2], 1 - at[3])) for at in every]
    a_pairs = [(place(*at), place(at[0], at[1], 1 - at[2], at[3])) for at in every]
    b_pairs = [(place(*at), place(at[0], 1 - at[1], at[2], at[3])) for at in every]
    groups = [
        [place(line, b, a, core) for line in range(lines)]
        for b in range(2)
        for a in range(2)
        for core in range(2)
    ]
    half = lines // 2

    def swap_core(value):
        return lax.ppermute(value, "dev", core_pairs)

    def swap_a(value):
        return lax.ppermute(value, "dev", a_pairs)

    def swap_b(value):
        return lax.ppermute(value, "dev", b_pairs)

    def body(
        tokens,
        lengths,
        out_grad,
        first_gain,
        first_shift,
        query_weight,
        query_bias,
        key_weight,
        value_weight,
        value_bias,
        proj_weight,
        proj_bias,
        mid_gain,
        mid_shift,
        up_weight,
        up_bias,
        down_weight,
        down_bias,
    ):
        position = lax.axis_index("dev")
        core = position % 2
        chip = position // 2
        at_a = chip % 2
        at_b = (chip // 2) % 2
        own_rows, width = tokens.shape
        rows = 2 * own_rows
        shard = query_weight.shape[0]
        side = width // 2
        hidden = up_weight.shape[1]
        block = hidden // devices
        part = block // 2
        spread = block // shard
        length = lax.dynamic_slice(lengths, (chip,), (1,))

        def both(own, other):
            first = jnp.where(core == 0, own, other)
            second = jnp.where(core == 0, other, own)
            return jnp.concatenate([first, second], axis=0)

        def columns(weight, which):
            return lax.dynamic_slice(weight, (0, which * side), (weight.shape[0], side))

        def blocks(weight, which):
            cut = weight.reshape(weight.shape[0], chips, 2, block)
            return lax.dynamic_index_in_dim(cut, which, 2, keepdims=False).reshape(
                weight.shape[0], chips * block
            )

        def after(value, *earlier):
            return lax.optimization_barrier((value, *earlier))[0]

        def gather_line(value):
            return lax.all_gather(value, "dev", axis=0, axis_index_groups=groups)

        def gather_near(line):
            return swap_a(line), swap_b(line)

        def gather_far(near):
            from_a, from_b = near
            return swap_a(from_b[:half]), swap_b(from_a[half:])

        plane = jnp.stack([at_a, at_b]).astype(jnp.int32)

        def ordered(index, own, other):
            return jnp.stack([jnp.where(index == 0, own, other), jnp.where(index == 0, other, own)])

        def gather_plane(value):
            value = ordered(at_a, value, swap_a(value))
            return ordered(at_b, value, swap_b(value))

        def parts_of(whole):
            parts = whole.reshape(lines, 2, 2, whole.shape[0] // chips, whole.shape[1])

            def pick(b, a):
                at = lax.dynamic_index_in_dim(parts, b, 1, keepdims=False)
                return lax.dynamic_index_in_dim(at, a, 1, keepdims=False)

            return pick

        def give_far(pick):
            far = pick(1 - at_b, 1 - at_a)
            return far[:half], far[half:]

        def scatter_far(pick):
            given = give_far(pick)
            return swap_a(given[0]), swap_b(given[1])

        def scatter_add(pick, far):
            far_low, far_high = far
            to_a = pick(at_b, 1 - at_a)
            to_b = pick(1 - at_b, at_a)
            to_a = jnp.concatenate([to_a[:half], to_a[half:] + far_high], axis=0)
            to_b = jnp.concatenate([to_b[:half] + far_low, to_b[half:]], axis=0)
            return to_a, to_b

        def scatter_near(given):
            return swap_a(given[0]), swap_b(given[1])

        def scatter_own(pick, near):
            own = pick(at_b, at_a).astype(F32) + near[0].astype(F32) + near[1].astype(F32)
            return own.astype(BF)

        def scatter_a(parts):
            own = lax.dynamic_index_in_dim(parts, at_a, 1, keepdims=False)
            return own + swap_a(lax.dynamic_index_in_dim(parts, 1 - at_a, 1, keepdims=False))

        def scatter_b(parts):
            own = lax.dynamic_index_in_dim(parts, at_b, 0, keepdims=False)
            return own + swap_b(lax.dynamic_index_in_dim(parts, 1 - at_b, 0, keepdims=False))

        def scatter_line(parts):
            return lax.psum_scatter(
                parts, "dev", scatter_dimension=0, axis_index_groups=groups
            )

        other = 1 - core
        vectors = jnp.stack(
            [first_gain, first_shift, query_bias, value_bias, proj_bias, mid_gain, mid_shift, down_bias],
            axis=1,
        )
        vectors = jnp.concatenate([vectors, up_bias.reshape(shard, spread)], axis=1)
        vectors = jnp.pad(vectors, ((0, 0), (0, VECTORS - vectors.shape[1])))
        own_qkv = jnp.concatenate(
            [columns(query_weight, core), columns(key_weight, core), columns(value_weight, core), vectors], axis=1
        )
        give_qkv = jnp.concatenate(
            [columns(query_weight, other), columns(key_weight, other), columns(value_weight, other), vectors], axis=1
        )
        qkv_shard = both(own_qkv, swap_core(give_qkv))
        all_tokens = both(tokens, swap_core(tokens)).astype(F32)
        tokens, up_weight, proj_weight = lax.optimization_barrier((tokens, up_weight, proj_weight, qkv_shard))[:3]

        def rest_columns(which):
            return jnp.concatenate([columns(proj_weight, which), blocks(up_weight, which)], axis=1)

        rest_shard = both(rest_columns(core), swap_core(rest_columns(other)))
        all_grad = both(out_grad, swap_core(out_grad))
        live = jnp.arange(rows) < length[0]
        grad_low = jnp.where(live[:, None], all_grad, jnp.zeros_like(all_grad))

        def put(whole, block_of, line_at, b, a):
            zero = jnp.int32(0)
            return lax.dynamic_update_slice(
                whole, block_of[:, None, None], (jnp.int32(line_at), b, a, zero, zero)
            )

        qkv_line = gather_line(qkv_shard)
        rest_line = gather_line(rest_shard)
        down_line = gather_line(down_weight)
        qkv_near = gather_near(qkv_line)
        from_a, from_b = qkv_near
        down_b_grad = 0.5 * jnp.sum(grad_low.astype(F32), axis=0)
        from_a, from_b, grad_low, down_b_grad = lax.optimization_barrier((from_a, from_b, grad_low, down_b_grad))
        given_far = (from_b[:half], from_a[half:])
        qkv_far = swap_a(given_far[0]), swap_b(given_far[1])
        rest_near = gather_near(after(rest_line, *given_far))
        w_qkv = jnp.zeros((lines, 2, 2, 2 * shard, 3 * side + VECTORS), BF)
        w_qkv = put(w_qkv, qkv_line, 0, at_b, at_a)
        w_qkv = put(w_qkv, from_a, 0, at_b, 1 - at_a)
        w_qkv = put(w_qkv, from_b, 0, 1 - at_b, at_a)
        w_qkv = put(w_qkv, qkv_far[0], 0, 1 - at_b, 1 - at_a)
        w_qkv = put(w_qkv, qkv_far[1], half, 1 - at_b, 1 - at_a)
        w_qkv = w_qkv.reshape(width, 3 * side + VECTORS)
        table = w_qkv[:, 3 * side :].astype(F32).T
        w_qkv = w_qkv[:, : 3 * side]
        gain_one, shift_one, b_query, b_value, b_proj, gain_two, shift_two, b_down = (
            table[i] for i in range(8)
        )
        hidden_bias = table[8 : 8 + spread].reshape(spread, chips, 2, shard)
        hidden_bias = lax.dynamic_index_in_dim(hidden_bias, core, 2, keepdims=False)
        hidden_bias = hidden_bias.transpose(1, 2, 0).reshape(chips * block)

        def rows_of(value, which):
            return lax.dynamic_slice(value, (which * own_rows, 0), (own_rows, value.shape[1]))

        def own_side(vector):
            return lax.dynamic_slice(vector, (core * side,), (side,))

        def normalize(value, gain, shift):
            center = value - jnp.mean(value, axis=-1, keepdims=True)
            spread_of = jnp.mean(center * center, axis=-1, keepdims=True)
            scale = lax.rsqrt(spread_of + EPS)
            hat = center * scale
            return hat * gain + shift, hat, scale

        def normalize_back(grad, hat, scale, gain):
            scaled = grad * gain
            mean = jnp.mean(scaled, axis=-1, keepdims=True)
            dot = jnp.mean(scaled * hat, axis=-1, keepdims=True)
            return (
                (scaled - mean - hat * dot) * scale,
                jnp.sum(grad * hat, axis=0),
                jnp.sum(grad, axis=0),
            )

        normed = normalize(all_tokens, gain_one, shift_one)[0].astype(BF)
        qkv_bias = jnp.concatenate([own_side(b_query), jnp.zeros((side,), F32), own_side(b_value)])
        qkv = (contract(w_qkv, normed, 0, 1) + qkv_bias[:, None]).astype(BF).reshape(3, side, rows)
        attended_own, log_total = attend(length, qkv)
        attended_own, down_line, *rest_near = lax.optimization_barrier((attended_own, down_line, *rest_near))
        rest_far = gather_far(rest_near)
        attended = both(attended_own, swap_core(attended_own))
        attended, *rest_far = lax.optimization_barrier((attended, *rest_far))
        down_near = gather_near(after(down_line, *rest_far))
        w_proj_side, w_up = join(plane, rest_line, rest_near, rest_far, (side, chips * block))
        w_proj_other = swap_core(w_proj_side)
        w_proj = jnp.concatenate(
            [
                jnp.where(core == 0, w_proj_side, w_proj_other),
                jnp.where(core == 0, w_proj_other, w_proj_side),
            ],
            axis=1,
        )
        mid = all_tokens + contract(attended, w_proj, 0, 0) + b_proj
        mid_normed, mid_hat, mid_scale = normalize(mid, gain_two, shift_two)
        mid_low = mid_normed.astype(BF)
        pre_act = contract(mid_low, w_up, 1, 0) + hidden_bias
        below = 0.5 + 0.5 * lax.erf(pre_act * math.sqrt(0.5))
        activ = (pre_act * below).astype(BF)
        slope = (below + pre_act * (jnp.exp(-0.5 * pre_act * pre_act) * (1.0 / math.sqrt(2.0 * math.pi)))).astype(BF)
        activ, slope, *down_near = lax.optimization_barrier((activ, slope, *down_near))
        down_far = gather_far(down_near)

        down_grad = contract(activ, grad_low, 0, 0).astype(BF).reshape(lines, 2, 2, 2, part, width)
        late_line = lax.psum_scatter(
            down_grad[:, :, :, 1], "dev", scatter_dimension=0, axis_index_groups=groups
        )
        down_pick = parts_of(down_grad[:, :, :, 0].reshape(chips * part, width))
        down_back_far = scatter_far(down_pick)
        w_down = join(plane, down_line, down_near, down_far, (width,))[0]
        w_down = after(w_down, down_grad)
        pre_grad = (contract(grad_low, w_down, 1, 1) * slope.astype(F32)).astype(BF)
        mid_part = contract(pre_grad, w_up, 1, 1).astype(BF)
        mid_other = swap_core(mid_part)
        down_back_far = lax.optimization_barrier((*down_back_far, mid_part))[:2]
        down_given = scatter_add(down_pick, down_back_far)
        down_back_near = scatter_near(down_given)
        up_grad = contract(after(mid_low, *down_given), pre_grad, 0, 0).astype(BF)
        up_pick = parts_of(up_grad)
        up_give = give_far(up_pick)
        up_far = swap_a(up_give[0]), swap_b(up_give[1])
        up_b_grad = jnp.sum(pre_grad.astype(F32), axis=0)
        mid_other, _, _ = lax.optimization_barrier((mid_other, *up_give))
        mid_grad, attended_grad, proj_grad, *mid_sums = norm_back(
            core.reshape(1).astype(jnp.int32), mid, mid_part, mid_other, grad_low, gain_two, w_proj, attended
        )
        mid_grad, attended_grad, proj_grad, *up_far = lax.optimization_barrier(
            (mid_grad, attended_grad, proj_grad, *up_far)
        )
        gain_two_grad, shift_two_grad, proj_b_grad = (0.5 * item[0] for item in mid_sums)
        up_given = scatter_add(up_pick, up_far)
        up_near = scatter_near(up_given)
        proj_line = lax.psum_scatter(
            proj_grad.reshape(lines, 2, 2, 2 * shard, side), "dev", scatter_dimension=0, axis_index_groups=groups
        )
        attended_grad, late_line = lax.optimization_barrier(
            (attended_grad, late_line, proj_grad, *up_given)
        )[:2]
        qkv_back = attend_back(length, qkv, attended_grad, log_total).reshape(3 * side, rows)
        qkv_back, *down_back_near = lax.optimization_barrier((qkv_back, *down_back_near))
        down_own = scatter_own(down_pick, down_back_near)
        down_sum = scatter_line(down_own)
        qkv_grad = contract(normed, qkv_back, 0, 1).astype(BF)
        qkv_pick = parts_of(qkv_grad)
        qkv_give = give_far(qkv_pick)
        qkv_far = swap_a(qkv_give[0]), swap_b(qkv_give[1])
        normed_part = contract(after(qkv_back, *qkv_give), w_qkv, 0, 1).astype(BF)
        normed_other = swap_core(rows_of(normed_part, other))
        normed_part, proj_line, *qkv_far = lax.optimization_barrier((normed_part, proj_line, *qkv_far))
        qkv_given = scatter_add(qkv_pick, qkv_far)
        qkv_near = scatter_near(qkv_given)
        up_near = lax.optimization_barrier((*up_near, *qkv_given))[:2]
        up_own = scatter_own(up_pick, up_near)
        qkv_b_grad = jnp.sum(qkv_back.astype(F32), axis=1)
        normed_part, down_sum, *_ = lax.optimization_barrier((normed_part, down_sum, up_own, *qkv_given))
        input_grad, gain_one_grad, shift_one_grad = first_back(
            core.reshape(1).astype(jnp.int32), tokens, normed_part, normed_other, mid_grad, gain_one
        )
        gain_one_grad, shift_one_grad = gain_one_grad[0], shift_one_grad[0]

        def on_side(vector):
            return lax.dynamic_update_slice(jnp.zeros((width,), F32), vector, (core * side,))

        up_rows = up_b_grad.reshape(chips, 1, shard, spread)
        up_rows = lax.dynamic_update_slice(
            jnp.zeros((chips, 2, shard, spread), F32), up_rows, (0, core, 0, 0)
        ).reshape(width, spread)
        sums = jnp.stack(
            [
                gain_one_grad,
                shift_one_grad,
                on_side(qkv_b_grad[:side]),
                on_side(qkv_b_grad[2 * side :]),
                proj_b_grad,
                gain_two_grad,
                shift_two_grad,
                down_b_grad,
            ],
            axis=1,
        )
        sums = jnp.concatenate([sums, up_rows], axis=1)
        sums = jnp.pad(sums, ((0, 0), (0, VECTORS - sums.shape[1]))).astype(BF)
        sums = after(sums, input_grad)
        sums = sums.reshape(lines, 2, 2, 2 * shard, VECTORS)

        def pick(b, a):
            at = lax.dynamic_index_in_dim(sums, b, 1, keepdims=False)
            return lax.dynamic_index_in_dim(at, a, 1, keepdims=False)

        def halves(parts, axis, at):
            own = lax.dynamic_index_in_dim(parts, at, axis, keepdims=False)
            return own, lax.dynamic_index_in_dim(parts, 1 - at, axis, keepdims=False)

        vector_come = swap_a(jnp.stack([pick(at_b, 1 - at_a), pick(1 - at_b, 1 - at_a)]))
        late_keep, late_give = halves(after(late_line, *qkv_given), 1, at_a)
        proj_keep, proj_give = halves(after(proj_line, *qkv_given), 1, at_a)
        late_come, proj_come = swap_a(late_give), swap_a(proj_give)
        up_sum = scatter_line(up_own)
        down_part = product(after(activ, up_own), w_down)
        down_part, vector_come, late_come, proj_come = lax.optimization_barrier(
            (down_part, vector_come, late_come, proj_come)
        )
        vector_near = swap_b(pick(1 - at_b, at_a) + vector_come[1])
        late_keep, late_give = halves(late_keep + late_come, 0, at_b)
        proj_keep, proj_give = halves(proj_keep + proj_come, 0, at_b)
        late_come, proj_come = swap_b(late_give), swap_b(proj_give)
        up_sum, *qkv_near = lax.optimization_barrier((up_sum, *qkv_near, late_give, proj_give))[:3]
        vector_own = pick(at_b, at_a) + vector_come[0] + vector_near
        own = jnp.concatenate([scatter_own(qkv_pick, qkv_near), vector_own], axis=2)
        qkv_sum = scatter_line(own)
        down_other = swap_core(rows_of(down_part, other))
        late_sum = late_keep + late_come
        proj_sum = proj_keep + proj_come
        output = (
            rows_of(mid, core) + rows_of(down_part, core).astype(F32) + down_other.astype(F32) + b_down
        ).astype(BF)

        def finish(sum_of, which):
            return lax.dynamic_slice(sum_of, (which * shard, 0), (shard, sum_of.shape[1]))

        def exchange(sum_of):
            mine = finish(sum_of, core)
            theirs = swap_core(finish(sum_of, other))
            left = jnp.where(core == 0, mine, theirs).astype(F32)
            right = jnp.where(core == 0, theirs, mine).astype(F32)
            return left, right

        proj_left, proj_right = exchange(proj_sum)
        up_left, up_right = exchange(after(up_sum, proj_left))
        up_all = jnp.stack(
            [
                up_left.reshape(shard, chips, block),
                up_right.reshape(shard, chips, block),
            ],
            axis=2,
        ).reshape(shard, hidden)
        down_sum = jnp.concatenate([down_sum, late_sum], axis=0)
        qkv_left, qkv_right = exchange(
            lax.optimization_barrier((qkv_sum, up_all, down_sum, output))[0]
        )

        def joined(left, right, start):
            return jnp.concatenate([left[:, start : start + side], right[:, start : start + side]], axis=1)

        at_vectors = slice(3 * side, 3 * side + 8 + spread)
        vector_rows = qkv_left[:, at_vectors] + qkv_right[:, at_vectors]
        return (
            output,
            input_grad,
            vector_rows[:, 0],
            vector_rows[:, 1],
            joined(qkv_left, qkv_right, 0),
            vector_rows[:, 2],
            joined(qkv_left, qkv_right, side),
            joined(qkv_left, qkv_right, 2 * side),
            vector_rows[:, 3],
            joined(proj_left, proj_right, 0),
            vector_rows[:, 4],
            vector_rows[:, 5],
            vector_rows[:, 6],
            up_all,
            vector_rows[:, 8 : 8 + spread].reshape(block),
            down_sum.astype(F32),
            vector_rows[:, 7],
        )

    return body


def solution(mesh):
    matrix, vector = P("dev", None), P("dev")
    return jax.shard_map(
        make_body(mesh.shape["dev"]),
        mesh=mesh,
        in_specs=(
            matrix,
            P(),
            matrix,
            vector,
            vector,
            matrix,
            vector,
            matrix,
            matrix,
            vector,
            matrix,
            vector,
            vector,
            vector,
            matrix,
            vector,
            matrix,
            vector,
        ),
        out_specs=(
            matrix,
            matrix,
            vector,
            vector,
            matrix,
            vector,
            matrix,
            matrix,
            vector,
            matrix,
            vector,
            vector,
            vector,
            matrix,
            vector,
            matrix,
            vector,
        ),
        check_vma=False,
    )
```

```python
import functools
import math

import jax
import jax.numpy as jnp
from jax import lax
from jax.experimental import pallas as pl
from jax.experimental.pallas import tpu as pltpu
from jax.sharding import PartitionSpec as P

HD = 80
EPS = 1e-05
NEG = -1e30
SCALE = HD**-0.5
LOG2E = math.log2(math.e)
BF = jnp.bfloat16
F32 = jnp.float32
VECTORS = 128
SMALL = pl.CostEstimate(flops=1, bytes_accessed=1, transcendentals=0)


def contract(left, right, left_dim, right_dim):
    return lax.dot_general(
        left, right, (((left_dim,), (right_dim,)), ((), ())), preferred_element_type=F32
    )


def attend_kernel(length, qkv, attended, log_total):
    rows = qkv.shape[2]
    keys = qkv[1].T
    dead = lax.broadcasted_iota(jnp.int32, (rows, 1), 0) >= length[0]
    scores = contract(keys, qkv[0], 1, 0) + jnp.where(dead, NEG, 0.0).astype(F32)
    top = jnp.max(scores, axis=0, keepdims=True)
    weights = jnp.exp2((scores - top) * (SCALE * LOG2E))
    total = jnp.sum(weights, axis=0, keepdims=True)
    probs = (weights * (1.0 / total)).astype(BF)
    attended[...] = contract(qkv[2], probs, 1, 0).astype(BF)
    log_total[0] = top * (SCALE * LOG2E) + jnp.log2(total)


def attend(length, qkv):
    _, width, rows = qkv.shape
    heads = width // HD
    return pl.pallas_call(
        attend_kernel,
        grid=(heads,),
        in_specs=[
            pl.BlockSpec(memory_space=pltpu.SMEM),
            pl.BlockSpec((3, HD, rows), lambda h: (0, h, 0)),
        ],
        out_specs=[
            pl.BlockSpec((HD, rows), lambda h: (h, 0)),
            pl.BlockSpec((1, 1, rows), lambda h: (h, 0, 0)),
        ],
        out_shape=[
            jax.ShapeDtypeStruct((width, rows), BF),
            jax.ShapeDtypeStruct((heads, 1, rows), F32),
        ],
        compiler_params=pltpu.CompilerParams(vmem_limit_bytes=40 << 20),
        cost_estimate=SMALL,
    )(length, qkv)


def attend_back_kernel(length, qkv, out_grad, log_total, grads, key_sum, value_sum, *, step):
    rows = qkv.shape[2]
    keys = qkv[1].T
    values = qkv[2].T
    dead = lax.broadcasted_iota(jnp.int32, (rows, 1), 0) >= length[0]
    bias = jnp.where(dead, NEG, 0.0).astype(F32)
    for at in range(0, rows, step):
        part = slice(at, at + step)
        queries = qkv[0, :, part]
        out_part = out_grad[:, part]
        scores = contract(keys, queries, 1, 0) + bias
        probs = jnp.exp2(scores * (SCALE * LOG2E) - log_total[0, :, part])
        prob_grad = contract(values, out_part, 1, 0)
        inner = jnp.sum(probs * prob_grad, axis=0, keepdims=True)
        score_grad = (probs * (prob_grad - inner)).astype(BF)
        probs_low = probs.astype(BF)
        grads[0, :, part] = (contract(qkv[1], score_grad, 1, 0) * SCALE).astype(BF)
        key_part = contract(queries, score_grad, 1, 1)
        value_part = contract(out_part, probs_low, 1, 1)
        if at == 0:
            key_sum[...] = key_part
            value_sum[...] = value_part
        else:
            key_sum[...] += key_part
            value_sum[...] += value_part
    grads[1] = (key_sum[...] * SCALE).astype(BF)
    grads[2] = value_sum[...].astype(BF)


def attend_back(length, qkv, out_grad, log_total):
    _, width, rows = qkv.shape
    heads = width // HD
    return pl.pallas_call(
        functools.partial(attend_back_kernel, step=min(512, rows)),
        grid=(heads,),
        in_specs=[
            pl.BlockSpec(memory_space=pltpu.SMEM),
            pl.BlockSpec((3, HD, rows), lambda h: (0, h, 0)),
            pl.BlockSpec((HD, rows), lambda h: (h, 0)),
            pl.BlockSpec((1, 1, rows), lambda h: (h, 0, 0)),
        ],
        out_specs=pl.BlockSpec((3, HD, rows), lambda h: (0, h, 0)),
        out_shape=jax.ShapeDtypeStruct((3, width, rows), BF),
        scratch_shapes=[pltpu.VMEM((HD, rows), F32), pltpu.VMEM((HD, rows), F32)],
        compiler_params=pltpu.CompilerParams(vmem_limit_bytes=48 << 20),
        cost_estimate=SMALL,
    )(length, qkv, out_grad, log_total)


def product_kernel(left, right, out):
    out[...] = contract(left[...], right[...], 1, 0).astype(BF)


def product(left, right):
    rows, depth = left.shape
    width = right.shape[1]
    return pl.pallas_call(
        product_kernel,
        grid=(width // 256,),
        in_specs=[
            pl.BlockSpec((rows, depth), lambda i: (0, 0), pipeline_mode=pl.Buffered(1)),
            pl.BlockSpec((depth, 256), lambda i: (0, i)),
        ],
        out_specs=pl.BlockSpec((rows, 256), lambda i: (0, i)),
        out_shape=jax.ShapeDtypeStruct((rows, width), BF),
        compiler_params=pltpu.CompilerParams(vmem_limit_bytes=16 << 20),
        cost_estimate=SMALL,
    )(left, right)


def norm_back_kernel(
    core, mid, part, other, grad, gain, heads, attended,
    mid_grad, attended_grad, proj_grad, gain_sum, shift_sum, branch_sum, total, held,
):
    at = pl.program_id(0)
    value = mid[...]
    center = value - jnp.mean(value, axis=-1, keepdims=True)
    scale = lax.rsqrt(jnp.mean(center * center, axis=-1, keepdims=True) + EPS)
    hat = center * scale
    error = part[...].astype(F32) + other[...].astype(F32)
    scaled = error * gain[...]
    mean = jnp.mean(scaled, axis=-1, keepdims=True)
    dot = jnp.mean(scaled * hat, axis=-1, keepdims=True)
    summed = grad[...].astype(F32) + (scaled - mean - hat * dot) * scale
    low = summed.astype(BF)
    mid_grad[...] = summed
    held[...] = low
    attended_grad[...] = contract(heads[...], low, 1, 1).astype(BF)
    side = proj_grad.shape[1]
    columns = held[:, pl.ds(pl.multiple_of(core[0] * side, 128), side)]

    @pl.when(at == 0)
    def _():
        total[...] = jnp.zeros_like(total)
        gain_sum[...] = jnp.zeros_like(gain_sum)
        shift_sum[...] = jnp.zeros_like(shift_sum)
        branch_sum[...] = jnp.zeros_like(branch_sum)

    total[...] += contract(attended[...], columns, 1, 0)
    gain_sum[...] += jnp.sum(error * hat, axis=0, keepdims=True)
    shift_sum[...] += jnp.sum(error, axis=0, keepdims=True)
    branch_sum[...] += jnp.sum(low.astype(F32), axis=0, keepdims=True)

    @pl.when(at == pl.num_programs(0) - 1)
    def _():
        proj_grad[...] = total[...].astype(BF)


def norm_back(core, mid, part, other, grad, gain, weight, attended):
    rows, width = mid.shape
    side = width // 2
    cut = 256
    row = pl.BlockSpec((cut, width), lambda i, core: (i, 0))
    one = pl.BlockSpec((1, width), lambda i, core: (0, 0))
    return pl.pallas_call(
        norm_back_kernel,
        grid_spec=pltpu.PrefetchScalarGridSpec(
            num_scalar_prefetch=1,
            grid=(rows // cut,),
            in_specs=[
                row,
                row,
                row,
                row,
                one,
                pl.BlockSpec((side, width), lambda i, core: (core[0], 0)),
                pl.BlockSpec((width, cut), lambda i, core: (0, i)),
            ],
            out_specs=[
                row,
                pl.BlockSpec((side, cut), lambda i, core: (0, i)),
                pl.BlockSpec((width, side), lambda i, core: (0, 0)),
                one,
                one,
                one,
            ],
            scratch_shapes=[pltpu.VMEM((width, side), F32), pltpu.VMEM((cut, width), BF)],
        ),
        out_shape=[
            jax.ShapeDtypeStruct((rows, width), F32),
            jax.ShapeDtypeStruct((side, rows), BF),
            jax.ShapeDtypeStruct((width, side), BF),
            jax.ShapeDtypeStruct((1, width), F32),
            jax.ShapeDtypeStruct((1, width), F32),
            jax.ShapeDtypeStruct((1, width), F32),
        ],
        compiler_params=pltpu.CompilerParams(vmem_limit_bytes=28 << 20),
        cost_estimate=SMALL,
    )(core, mid, part, other, grad, gain.reshape(1, width), weight, attended)


def first_back_kernel(core, tokens, part, other, mid_grad, gain, grad, gain_sum, shift_sum):
    value = tokens[...].astype(F32)
    center = value - jnp.mean(value, axis=-1, keepdims=True)
    scale = lax.rsqrt(jnp.mean(center * center, axis=-1, keepdims=True) + EPS)
    hat = center * scale
    error = part[...].astype(F32) + other[...].astype(F32)
    scaled = error * gain[...]
    mean = jnp.mean(scaled, axis=-1, keepdims=True)
    dot = jnp.mean(scaled * hat, axis=-1, keepdims=True)
    grad[...] = (mid_grad[...] + (scaled - mean - hat * dot) * scale).astype(BF)

    @pl.when(pl.program_id(0) == 0)
    def _():
        gain_sum[...] = jnp.zeros_like(gain_sum)
        shift_sum[...] = jnp.zeros_like(shift_sum)

    gain_sum[...] += jnp.sum(error * hat, axis=0, keepdims=True)
    shift_sum[...] += jnp.sum(error, axis=0, keepdims=True)


def first_back(core, tokens, part, other, mid_grad, gain):
    rows, width = tokens.shape
    cut = 256
    steps = rows // cut
    own = pl.BlockSpec((cut, width), lambda i, core: (i, 0))
    mine = pl.BlockSpec((cut, width), lambda i, core: (core[0] * steps + i, 0))
    one = pl.BlockSpec((1, width), lambda i, core: (0, 0))
    return pl.pallas_call(
        first_back_kernel,
        grid_spec=pltpu.PrefetchScalarGridSpec(
            num_scalar_prefetch=1,
            grid=(steps,),
            in_specs=[own, mine, own, mine, one],
            out_specs=[own, one, one],
        ),
        out_shape=[
            jax.ShapeDtypeStruct((rows, width), BF),
            jax.ShapeDtypeStruct((1, width), F32),
            jax.ShapeDtypeStruct((1, width), F32),
        ],
        compiler_params=pltpu.CompilerParams(vmem_limit_bytes=20 << 20),
        cost_estimate=SMALL,
    )(core, tokens, part, other, mid_grad, gain.reshape(1, width))


def join_kernel(plane, line, from_a, from_b, far_low, far_high, *wholes):
    turn, at = pl.program_id(0), pl.program_id(1)
    half = pl.num_programs(1) // 2

    def put(source):
        start = 0
        for whole in wholes:
            stop = start + whole.shape[-1]
            whole[0, 0, 0] = source[0, :, start:stop]
            start = stop

    pl.when(turn == 0)(lambda: put(line))
    pl.when(turn == 1)(lambda: put(from_a))
    pl.when(turn == 2)(lambda: put(from_b))
    pl.when((turn == 3) & (at < half))(lambda: put(far_low))
    pl.when((turn == 3) & (at >= half))(lambda: put(far_high))


def join(plane, line, near, far, cuts):
    lines, shard, width = line.shape
    half = lines // 2

    def source(turn_of):
        def at(turn, i, plane):
            return (jnp.where(turn == turn_of, i, jnp.where(turn < turn_of, 0, lines - 1)), 0, 0)

        return pl.BlockSpec((1, shard, width), at)

    def low(turn, i, plane):
        return (jnp.where(turn == 3, jnp.minimum(i, half - 1), 0), 0, 0)

    def high(turn, i, plane):
        return (jnp.where(turn == 3, jnp.maximum(i - half, 0), 0), 0, 0)

    def target(turn, i, plane):
        a, b = plane[0], plane[1]
        return (i, jnp.where(turn >= 2, 1 - b, b), jnp.where(turn % 2 == 1, 1 - a, a), 0, 0)

    wholes = pl.pallas_call(
        join_kernel,
        grid_spec=pltpu.PrefetchScalarGridSpec(
            num_scalar_prefetch=1,
            grid=(4, lines),
            in_specs=[
                source(0),
                source(1),
                source(2),
                pl.BlockSpec((1, shard, width), low),
                pl.BlockSpec((1, shard, width), high),
            ],
            out_specs=[pl.BlockSpec((1, 1, 1, shard, cut), target) for cut in cuts],
        ),
        out_shape=[jax.ShapeDtypeStruct((lines, 2, 2, shard, cut), line.dtype) for cut in cuts],
        compiler_params=pltpu.CompilerParams(vmem_limit_bytes=24 << 20),
        cost_estimate=SMALL,
    )(plane, line, *near, *far)
    return [whole.reshape(lines * 4 * shard, whole.shape[-1]) for whole in wholes]


def make_body(devices):
    chips = devices // 2
    lines = chips // 4

    def place(line, b, a, core):
        return ((line * 2 + b) * 2 + a) * 2 + core

    every = [
        (line, b, a, core)
        for line in range(lines)
        for b in range(2)
        for a in range(2)
        for core in range(2)
    ]
    core_pairs = [(place(*at), place(at[0], at[1], at[2], 1 - at[3])) for at in every]
    a_pairs = [(place(*at), place(at[0], at[1], 1 - at[2], at[3])) for at in every]
    b_pairs = [(place(*at), place(at[0], 1 - at[1], at[2], at[3])) for at in every]
    groups = [
        [place(line, b, a, core) for line in range(lines)]
        for b in range(2)
        for a in range(2)
        for core in range(2)
    ]
    half = lines // 2

    def swap_core(value):
        return lax.ppermute(value, "dev", core_pairs)

    def swap_a(value):
        return lax.ppermute(value, "dev", a_pairs)

    def swap_b(value):
        return lax.ppermute(value, "dev", b_pairs)

    def body(
        tokens,
        lengths,
        out_grad,
        first_gain,
        first_shift,
        query_weight,
        query_bias,
        key_weight,
        value_weight,
        value_bias,
        proj_weight,
        proj_bias,
        mid_gain,
        mid_shift,
        up_weight,
        up_bias,
        down_weight,
        down_bias,
    ):
        position = lax.axis_index("dev")
        core = position % 2
        chip = position // 2
        at_a = chip % 2
        at_b = (chip // 2) % 2
        own_rows, width = tokens.shape
        rows = 2 * own_rows
        shard = query_weight.shape[0]
        side = width // 2
        hidden = up_weight.shape[1]
        block = hidden // devices
        part = block // 2
        spread = block // shard
        length = lax.dynamic_slice(lengths, (chip,), (1,))

        def both(own, other):
            first = jnp.where(core == 0, own, other)
            second = jnp.where(core == 0, other, own)
            return jnp.concatenate([first, second], axis=0)

        def columns(weight, which):
            return lax.dynamic_slice(weight, (0, which * side), (weight.shape[0], side))

        def blocks(weight, which):
            cut = weight.reshape(weight.shape[0], chips, 2, block)
            return lax.dynamic_index_in_dim(cut, which, 2, keepdims=False).reshape(
                weight.shape[0], chips * block
            )

        def after(value, *earlier):
            return lax.optimization_barrier((value, *earlier))[0]

        def gather_line(value):
            return lax.all_gather(value, "dev", axis=0, axis_index_groups=groups)

        def gather_near(line):
            return swap_a(line), swap_b(line)

        def gather_far(near):
            from_a, from_b = near
            return swap_a(from_b[:half]), swap_b(from_a[half:])

        plane = jnp.stack([at_a, at_b]).astype(jnp.int32)

        def ordered(index, own, other):
            return jnp.stack([jnp.where(index == 0, own, other), jnp.where(index == 0, other, own)])

        def gather_plane(value):
            value = ordered(at_a, value, swap_a(value))
            return ordered(at_b, value, swap_b(value))

        def parts_of(whole):
            parts = whole.reshape(lines, 2, 2, whole.shape[0] // chips, whole.shape[1])

            def pick(b, a):
                at = lax.dynamic_index_in_dim(parts, b, 1, keepdims=False)
                return lax.dynamic_index_in_dim(at, a, 1, keepdims=False)

            return pick

        def give_far(pick):
            far = pick(1 - at_b, 1 - at_a)
            return far[:half], far[half:]

        def scatter_far(pick):
            given = give_far(pick)
            return swap_a(given[0]), swap_b(given[1])

        def scatter_add(pick, far):
            far_low, far_high = far
            to_a = pick(at_b, 1 - at_a)
            to_b = pick(1 - at_b, at_a)
            to_a = jnp.concatenate([to_a[:half], to_a[half:] + far_high], axis=0)
            to_b = jnp.concatenate([to_b[:half] + far_low, to_b[half:]], axis=0)
            return to_a, to_b

        def scatter_near(given):
            return swap_a(given[0]), swap_b(given[1])

        def scatter_own(pick, near):
            own = pick(at_b, at_a).astype(F32) + near[0].astype(F32) + near[1].astype(F32)
            return own.astype(BF)

        def scatter_a(parts):
            own = lax.dynamic_index_in_dim(parts, at_a, 1, keepdims=False)
            return own + swap_a(lax.dynamic_index_in_dim(parts, 1 - at_a, 1, keepdims=False))

        def scatter_b(parts):
            own = lax.dynamic_index_in_dim(parts, at_b, 0, keepdims=False)
            return own + swap_b(lax.dynamic_index_in_dim(parts, 1 - at_b, 0, keepdims=False))

        def scatter_line(parts):
            return lax.psum_scatter(
                parts, "dev", scatter_dimension=0, axis_index_groups=groups
            )

        other = 1 - core
        vectors = jnp.stack(
            [first_gain, first_shift, query_bias, value_bias, proj_bias, mid_gain, mid_shift, down_bias],
            axis=1,
        )
        vectors = jnp.concatenate([vectors, up_bias.reshape(shard, spread)], axis=1)
        vectors = jnp.pad(vectors, ((0, 0), (0, VECTORS - vectors.shape[1])))
        own_qkv = jnp.concatenate(
            [columns(query_weight, core), columns(key_weight, core), columns(value_weight, core), vectors, columns(proj_weight, core)],
            axis=1,
        )
        give_qkv = jnp.concatenate(
            [columns(query_weight, other), columns(key_weight, other), columns(value_weight, other), vectors, columns(proj_weight, other)],
            axis=1,
        )
        qkv_shard = both(own_qkv, swap_core(give_qkv))
        all_tokens = both(tokens, swap_core(tokens)).astype(F32)
        tokens, up_weight = lax.optimization_barrier((tokens, up_weight, qkv_shard))[:2]
        rest_shard = both(blocks(up_weight, core), swap_core(blocks(up_weight, other)))
        all_grad = both(out_grad, swap_core(out_grad))
        live = jnp.arange(rows) < length[0]
        grad_low = jnp.where(live[:, None], all_grad, jnp.zeros_like(all_grad))

        def put(whole, block_of, line_at, b, a):
            zero = jnp.int32(0)
            return lax.dynamic_update_slice(
                whole, block_of[:, None, None], (jnp.int32(line_at), b, a, zero, zero)
            )

        qkv_line = gather_line(qkv_shard)
        rest_line = gather_line(rest_shard)
        down_plane = gather_plane(after(down_weight, qkv_shard))
        w_down = gather_line(down_plane).reshape(chips * block, width)
        qkv_near = gather_near(after(qkv_line, down_plane))
        from_a, from_b = qkv_near
        down_b_grad = 0.5 * jnp.sum(grad_low.astype(F32), axis=0)
        from_a, from_b, grad_low, down_b_grad = lax.optimization_barrier((from_a, from_b, grad_low, down_b_grad))
        given_far = (from_b[:half], from_a[half:])
        qkv_far = swap_a(given_far[0]), swap_b(given_far[1])
        rest_near = gather_near(after(rest_line, *given_far))
        w_qkv = jnp.zeros((lines, 2, 2, 2 * shard, 4 * side + VECTORS), BF)
        w_qkv = put(w_qkv, qkv_line, 0, at_b, at_a)
        w_qkv = put(w_qkv, from_a, 0, at_b, 1 - at_a)
        w_qkv = put(w_qkv, from_b, 0, 1 - at_b, at_a)
        w_qkv = put(w_qkv, qkv_far[0], 0, 1 - at_b, 1 - at_a)
        w_qkv = put(w_qkv, qkv_far[1], half, 1 - at_b, 1 - at_a)
        w_qkv = w_qkv.reshape(width, 4 * side + VECTORS)
        table = w_qkv[:, 3 * side : 3 * side + VECTORS].astype(F32).T
        w_proj_side = w_qkv[:, 3 * side + VECTORS :]
        w_qkv = w_qkv[:, : 3 * side]
        gain_one, shift_one, b_query, b_value, b_proj, gain_two, shift_two, b_down = (
            table[i] for i in range(8)
        )
        hidden_bias = table[8 : 8 + spread].reshape(spread, chips, 2, shard)
        hidden_bias = lax.dynamic_index_in_dim(hidden_bias, core, 2, keepdims=False)
        hidden_bias = hidden_bias.transpose(1, 2, 0).reshape(chips * block)

        def rows_of(value, which):
            return lax.dynamic_slice(value, (which * own_rows, 0), (own_rows, value.shape[1]))

        def own_side(vector):
            return lax.dynamic_slice(vector, (core * side,), (side,))

        def normalize(value, gain, shift):
            center = value - jnp.mean(value, axis=-1, keepdims=True)
            spread_of = jnp.mean(center * center, axis=-1, keepdims=True)
            scale = lax.rsqrt(spread_of + EPS)
            hat = center * scale
            return hat * gain + shift, hat, scale

        def normalize_back(grad, hat, scale, gain):
            scaled = grad * gain
            mean = jnp.mean(scaled, axis=-1, keepdims=True)
            dot = jnp.mean(scaled * hat, axis=-1, keepdims=True)
            return (
                (scaled - mean - hat * dot) * scale,
                jnp.sum(grad * hat, axis=0),
                jnp.sum(grad, axis=0),
            )

        normed = normalize(all_tokens, gain_one, shift_one)[0].astype(BF)
        qkv_bias = jnp.concatenate([own_side(b_query), jnp.zeros((side,), F32), own_side(b_value)])
        qkv = (contract(w_qkv[:, : 3 * side], normed, 0, 1) + qkv_bias[:, None]).astype(BF).reshape(3, side, rows)
        attended_own, log_total = attend(length, qkv)
        attended_own, *rest_near = lax.optimization_barrier((attended_own, *rest_near))
        rest_far = gather_far(rest_near)
        attended = both(attended_own, swap_core(attended_own))
        w_proj_other = swap_core(w_proj_side)
        w_proj = jnp.concatenate(
            [
                jnp.where(core == 0, w_proj_side, w_proj_other),
                jnp.where(core == 0, w_proj_other, w_proj_side),
            ],
            axis=1,
        )
        mid = all_tokens + contract(attended, w_proj, 0, 0) + b_proj
        mid_normed, mid_hat, mid_scale = normalize(mid, gain_two, shift_two)
        mid_low = mid_normed.astype(BF)
        mid, mid_low, *rest_far = lax.optimization_barrier((mid, mid_low, *rest_far))
        w_up = join(plane, rest_line, rest_near, rest_far, (chips * block,))[0]
        pre_act = contract(mid_low, w_up, 1, 0) + hidden_bias
        below = 0.5 + 0.5 * lax.erf(pre_act * math.sqrt(0.5))
        activ = (pre_act * below).astype(BF)
        slope = (below + pre_act * (jnp.exp(-0.5 * pre_act * pre_act) * (1.0 / math.sqrt(2.0 * math.pi)))).astype(BF)
        activ, slope = lax.optimization_barrier((activ, slope))

        down_grad = contract(activ, grad_low, 0, 0).astype(BF)
        late_line = lax.psum_scatter(
            down_grad.reshape(lines, 2, 2, block, width), "dev", scatter_dimension=0, axis_index_groups=groups
        )
        w_down = after(w_down, down_grad)
        pre_grad = (contract(grad_low, w_down, 1, 1) * slope.astype(F32)).astype(BF)
        mid_part = contract(pre_grad, w_up, 1, 1).astype(BF)
        mid_other = swap_core(mid_part)
        up_grad = contract(after(mid_low, mid_part), pre_grad, 0, 0).astype(BF)
        up_pick = parts_of(up_grad)
        up_give = give_far(up_pick)
        up_far = swap_a(up_give[0]), swap_b(up_give[1])
        up_b_grad = jnp.sum(pre_grad.astype(F32), axis=0)
        mid_other, _, _ = lax.optimization_barrier((mid_other, *up_give))
        mid_grad, attended_grad, proj_grad, *mid_sums = norm_back(
            core.reshape(1).astype(jnp.int32), mid, mid_part, mid_other, grad_low, gain_two, w_proj, attended
        )
        mid_grad, attended_grad, proj_grad, *up_far = lax.optimization_barrier(
            (mid_grad, attended_grad, proj_grad, *up_far)
        )
        gain_two_grad, shift_two_grad, proj_b_grad = (0.5 * item[0] for item in mid_sums)
        up_given = scatter_add(up_pick, up_far)
        up_near = scatter_near(up_given)
        proj_pick = parts_of(proj_grad)
        proj_give = give_far(proj_pick)
        proj_far = swap_a(proj_give[0]), swap_b(proj_give[1])
        proj_far = lax.optimization_barrier((*proj_far, *up_given))[:2]
        proj_given = scatter_add(proj_pick, proj_far)
        proj_near = scatter_near(proj_given)
        attended_grad = after(attended_grad, *proj_given, *up_given)
        qkv_back = attend_back(length, qkv, attended_grad, log_total).reshape(3 * side, rows)
        qkv_back, *proj_near = lax.optimization_barrier((qkv_back, *proj_near))
        qkv_grad = contract(normed, qkv_back, 0, 1).astype(BF)
        qkv_pick = parts_of(qkv_grad)
        qkv_give = give_far(qkv_pick)
        qkv_far = swap_a(qkv_give[0]), swap_b(qkv_give[1])
        normed_part = contract(after(qkv_back, *qkv_give), w_qkv[:, : 3 * side], 0, 1).astype(BF)
        normed_other = swap_core(rows_of(normed_part, other))
        up_near = lax.optimization_barrier((*up_near, normed_part))[:2]
        up_own = scatter_own(up_pick, up_near)
        up_sum = scatter_line(up_own)
        normed_part, up_own, late_line, *qkv_far = lax.optimization_barrier((normed_part, up_own, late_line, *qkv_far))
        qkv_given = scatter_add(qkv_pick, qkv_far)
        qkv_near = scatter_near(qkv_given)
        down_part = product(after(activ, *qkv_given), w_down)
        qkv_b_grad = jnp.sum(qkv_back.astype(F32), axis=1)
        normed_part, *_ = lax.optimization_barrier((normed_part, *qkv_given))
        input_grad, gain_one_grad, shift_one_grad = first_back(
            core.reshape(1).astype(jnp.int32), tokens, normed_part, normed_other, mid_grad, gain_one
        )
        gain_one_grad, shift_one_grad = gain_one_grad[0], shift_one_grad[0]

        def on_side(vector):
            return lax.dynamic_update_slice(jnp.zeros((width,), F32), vector, (core * side,))

        up_rows = up_b_grad.reshape(chips, 1, shard, spread)
        up_rows = lax.dynamic_update_slice(
            jnp.zeros((chips, 2, shard, spread), F32), up_rows, (0, core, 0, 0)
        ).reshape(width, spread)
        sums = jnp.stack(
            [
                gain_one_grad,
                shift_one_grad,
                on_side(qkv_b_grad[:side]),
                on_side(qkv_b_grad[2 * side :]),
                proj_b_grad,
                gain_two_grad,
                shift_two_grad,
                down_b_grad,
            ],
            axis=1,
        )
        sums = jnp.concatenate([sums, up_rows], axis=1)
        sums = jnp.pad(sums, ((0, 0), (0, VECTORS - sums.shape[1]))).astype(BF)
        sums = after(sums, input_grad)
        sums = sums.reshape(lines, 2, 2, 2 * shard, VECTORS)

        def pick(b, a):
            at = lax.dynamic_index_in_dim(sums, b, 1, keepdims=False)
            return lax.dynamic_index_in_dim(at, a, 1, keepdims=False)

        def halves(parts, axis, at):
            own = lax.dynamic_index_in_dim(parts, at, axis, keepdims=False)
            return own, lax.dynamic_index_in_dim(parts, 1 - at, axis, keepdims=False)

        vector_come = swap_a(jnp.stack([pick(at_b, 1 - at_a), pick(1 - at_b, 1 - at_a)]))
        down_part, sums, vector_come, *qkv_near = lax.optimization_barrier((down_part, sums, vector_come, *qkv_near))
        vector_near = swap_b(pick(1 - at_b, at_a) + vector_come[1])
        qkv_own = scatter_own(qkv_pick, qkv_near)
        vector_own = pick(at_b, at_a) + vector_come[0] + vector_near
        proj_own = scatter_own(proj_pick, lax.optimization_barrier((*proj_near, *qkv_given))[:2])
        own = jnp.concatenate([qkv_own, vector_own, proj_own], axis=2)
        qkv_sum = scatter_line(own)
        late_keep, late_give = halves(after(late_line, own), 1, at_a)
        late_keep, late_give = halves(late_keep + swap_a(late_give), 0, at_b)
        down_other = swap_core(rows_of(down_part, other))
        late_sum = late_keep + swap_b(late_give)
        output = (
            rows_of(mid, core) + rows_of(down_part, core).astype(F32) + down_other.astype(F32) + b_down
        ).astype(BF)

        def finish(sum_of, which):
            return lax.dynamic_slice(sum_of, (which * shard, 0), (shard, sum_of.shape[1]))

        def exchange(sum_of):
            mine = finish(sum_of, core)
            theirs = swap_core(finish(sum_of, other))
            left = jnp.where(core == 0, mine, theirs).astype(F32)
            right = jnp.where(core == 0, theirs, mine).astype(F32)
            return left, right

        up_left, up_right = exchange(up_sum)
        up_all = jnp.stack(
            [
                up_left.reshape(shard, chips, block),
                up_right.reshape(shard, chips, block),
            ],
            axis=2,
        ).reshape(shard, hidden)
        down_sum = late_sum
        qkv_left, qkv_right = exchange(
            lax.optimization_barrier((qkv_sum, up_all, down_sum, output))[0]
        )

        def joined(left, right, start):
            return jnp.concatenate([left[:, start : start + side], right[:, start : start + side]], axis=1)

        at_vectors = slice(3 * side, 3 * side + 8 + spread)
        vector_rows = qkv_left[:, at_vectors] + qkv_right[:, at_vectors]
        return (
            output,
            input_grad,
            vector_rows[:, 0],
            vector_rows[:, 1],
            joined(qkv_left, qkv_right, 0),
            vector_rows[:, 2],
            joined(qkv_left, qkv_right, side),
            joined(qkv_left, qkv_right, 2 * side),
            vector_rows[:, 3],
            joined(qkv_left, qkv_right, 3 * side + VECTORS),
            vector_rows[:, 4],
            vector_rows[:, 5],
            vector_rows[:, 6],
            up_all,
            vector_rows[:, 8 : 8 + spread].reshape(block),
            down_sum.astype(F32),
            vector_rows[:, 7],
        )

    return body


def solution(mesh):
    matrix, vector = P("dev", None), P("dev")
    return jax.shard_map(
        make_body(mesh.shape["dev"]),
        mesh=mesh,
        in_specs=(
            matrix,
            P(),
            matrix,
            vector,
            vector,
            matrix,
            vector,
            matrix,
            matrix,
            vector,
            matrix,
            vector,
            vector,
            vector,
            matrix,
            vector,
            matrix,
            vector,
        ),
        out_specs=(
            matrix,
            matrix,
            vector,
            vector,
            matrix,
            vector,
            matrix,
            matrix,
            vector,
            matrix,
            vector,
            vector,
            vector,
            matrix,
            vector,
            matrix,
            vector,
        ),
        check_vma=False,
    )
```

```python
import functools
import math

import jax
import jax.numpy as jnp
from jax import lax
from jax.experimental import pallas as pl
from jax.experimental.pallas import tpu as pltpu
from jax.sharding import PartitionSpec as P

HD = 80
EPS = 1e-05
NEG = -1e30
SCALE = HD**-0.5
LOG2E = math.log2(math.e)
BF = jnp.bfloat16
F32 = jnp.float32
VECTORS = 128
PAD = 16
SMALL = pl.CostEstimate(flops=1, bytes_accessed=1, transcendentals=0)


def contract(left, right, left_dim, right_dim):
    return lax.dot_general(
        left, right, (((left_dim,), (right_dim,)), ((), ())), preferred_element_type=F32
    )


def attend_kernel(length, qkv, attended, log_total):
    rows = qkv.shape[2]
    keys = qkv[1].T
    dead = lax.broadcasted_iota(jnp.int32, (rows, 1), 0) >= length[0]
    scores = contract(keys, qkv[0], 1, 0) + jnp.where(dead, NEG, 0.0).astype(F32)
    top = jnp.max(scores, axis=0, keepdims=True)
    weights = jnp.exp2((scores - top) * (SCALE * LOG2E))
    total = jnp.sum(weights, axis=0, keepdims=True)
    probs = (weights * (1.0 / total)).astype(BF)
    attended[...] = contract(qkv[2], probs, 1, 0).astype(BF)
    log_total[0] = top * (SCALE * LOG2E) + jnp.log2(total)


def attend(length, qkv):
    _, width, rows = qkv.shape
    heads = width // HD
    return pl.pallas_call(
        attend_kernel,
        grid=(heads,),
        in_specs=[
            pl.BlockSpec(memory_space=pltpu.SMEM),
            pl.BlockSpec((3, HD, rows), lambda h: (0, h, 0)),
        ],
        out_specs=[
            pl.BlockSpec((HD, rows), lambda h: (h, 0)),
            pl.BlockSpec((1, 1, rows), lambda h: (h, 0, 0)),
        ],
        out_shape=[
            jax.ShapeDtypeStruct((width, rows), BF),
            jax.ShapeDtypeStruct((heads, 1, rows), F32),
        ],
        compiler_params=pltpu.CompilerParams(vmem_limit_bytes=40 << 20),
        cost_estimate=SMALL,
    )(length, qkv)


def term_rows(row, first):
    high = row.astype(BF).astype(F32)
    middle = (row - high).astype(BF).astype(F32)
    at = lax.broadcasted_iota(jnp.int32, (PAD, row.shape[1]), 0)
    terms = jnp.where(at == 1, high, jnp.where(at == 2, middle, jnp.where(at == 3, row - high - middle, 0.0)))
    return jnp.where(at == 0, first, terms).astype(BF)


def attend_back_kernel(length, qkv, out_grad, log_total, grads):
    rows = qkv.shape[2]
    at = lax.broadcasted_iota(jnp.int32, (rows, PAD), 1)
    dead = lax.broadcasted_iota(jnp.int32, (rows, PAD), 0) >= length[0]
    ones = jnp.where((at > 0) & (at < 4), 1.0, 0.0)
    mask = jnp.where((at == 0) & dead, NEG, ones)
    queries, out_part = qkv[0], out_grad[...]
    keys = jnp.concatenate([qkv[1].T, mask.astype(BF)], axis=1)
    query_terms = jnp.concatenate([queries, term_rows(log_total[0] * (-1.0 / (SCALE * LOG2E)), 1.0)], axis=0)
    probs = jnp.exp2(contract(keys, query_terms, 1, 0) * (SCALE * LOG2E))
    prob_grad = contract(qkv[2].T, out_part, 1, 0)
    inner = jnp.sum(probs * prob_grad, axis=0, keepdims=True)
    score_grad = (probs * (prob_grad - inner)).astype(BF)
    grads[0] = (contract(qkv[1], score_grad, 1, 0) * SCALE).astype(BF)
    grads[1] = (contract(score_grad, queries.T, 1, 0) * SCALE).astype(BF).T
    grads[2] = contract(probs.astype(BF), out_part.T, 1, 0).astype(BF).T


def attend_back(length, qkv, out_grad, log_total):
    _, width, rows = qkv.shape
    heads = width // HD
    head = pl.BlockSpec((HD, rows), lambda h: (h, 0))
    triple = pl.BlockSpec((3, HD, rows), lambda h: (0, h, 0))
    return pl.pallas_call(
        attend_back_kernel,
        grid=(heads,),
        in_specs=[
            pl.BlockSpec(memory_space=pltpu.SMEM),
            triple,
            head,
            pl.BlockSpec((1, 1, rows), lambda h: (h, 0, 0)),
        ],
        out_specs=triple,
        out_shape=jax.ShapeDtypeStruct((3, width, rows), BF),
        compiler_params=pltpu.CompilerParams(vmem_limit_bytes=24 << 20),
        cost_estimate=SMALL,
    )(length, qkv, out_grad, log_total)


def product_kernel(left, right, out):
    out[...] = contract(left[...], right[...], 1, 0).astype(BF)


def product(left, right):
    rows, depth = left.shape
    width = right.shape[1]
    return pl.pallas_call(
        product_kernel,
        grid=(width // 256,),
        in_specs=[
            pl.BlockSpec((rows, depth), lambda i: (0, 0), pipeline_mode=pl.Buffered(1)),
            pl.BlockSpec((depth, 256), lambda i: (0, i)),
        ],
        out_specs=pl.BlockSpec((rows, 256), lambda i: (0, i)),
        out_shape=jax.ShapeDtypeStruct((rows, width), BF),
        compiler_params=pltpu.CompilerParams(vmem_limit_bytes=60 << 20),
        cost_estimate=SMALL,
    )(left, right)


def norm_back_kernel(
    core, mid, part, other, grad, gain, heads, attended,
    mid_grad, attended_grad, proj_grad, gain_sum, shift_sum, branch_sum, total, held,
):
    at = pl.program_id(0)
    value = mid[...]
    center = value - jnp.mean(value, axis=-1, keepdims=True)
    scale = lax.rsqrt(jnp.mean(center * center, axis=-1, keepdims=True) + EPS)
    hat = center * scale
    error = part[...].astype(F32) + other[...].astype(F32)
    scaled = error * gain[...]
    mean = jnp.mean(scaled, axis=-1, keepdims=True)
    dot = jnp.mean(scaled * hat, axis=-1, keepdims=True)
    summed = grad[...].astype(F32) + (scaled - mean - hat * dot) * scale
    low = summed.astype(BF)
    mid_grad[...] = summed
    held[...] = low
    attended_grad[...] = contract(heads[...], low, 1, 1).astype(BF)
    side = proj_grad.shape[1]
    columns = held[:, pl.ds(pl.multiple_of(core[0] * side, 128), side)]

    @pl.when(at == 0)
    def _():
        total[...] = jnp.zeros_like(total)
        gain_sum[...] = jnp.zeros_like(gain_sum)
        shift_sum[...] = jnp.zeros_like(shift_sum)
        branch_sum[...] = jnp.zeros_like(branch_sum)

    total[...] += contract(attended[...], columns, 1, 0)
    gain_sum[...] += jnp.sum(error * hat, axis=0, keepdims=True)
    shift_sum[...] += jnp.sum(error, axis=0, keepdims=True)
    branch_sum[...] += jnp.sum(low.astype(F32), axis=0, keepdims=True)

    @pl.when(at == pl.num_programs(0) - 1)
    def _():
        proj_grad[...] = total[...].astype(BF)


def norm_back(core, mid, part, other, grad, gain, weight, attended):
    rows, width = mid.shape
    side = width // 2
    cut = 256
    row = pl.BlockSpec((cut, width), lambda i, core: (i, 0))
    one = pl.BlockSpec((1, width), lambda i, core: (0, 0))
    return pl.pallas_call(
        norm_back_kernel,
        grid_spec=pltpu.PrefetchScalarGridSpec(
            num_scalar_prefetch=1,
            grid=(rows // cut,),
            in_specs=[
                row,
                row,
                row,
                row,
                one,
                pl.BlockSpec((side, width), lambda i, core: (core[0], 0)),
                pl.BlockSpec((width, cut), lambda i, core: (0, i)),
            ],
            out_specs=[
                row,
                pl.BlockSpec((side, cut), lambda i, core: (0, i)),
                pl.BlockSpec((width, side), lambda i, core: (0, 0)),
                one,
                one,
                one,
            ],
            scratch_shapes=[pltpu.VMEM((width, side), F32), pltpu.VMEM((cut, width), BF)],
        ),
        out_shape=[
            jax.ShapeDtypeStruct((rows, width), F32),
            jax.ShapeDtypeStruct((side, rows), BF),
            jax.ShapeDtypeStruct((width, side), BF),
            jax.ShapeDtypeStruct((1, width), F32),
            jax.ShapeDtypeStruct((1, width), F32),
            jax.ShapeDtypeStruct((1, width), F32),
        ],
        compiler_params=pltpu.CompilerParams(vmem_limit_bytes=44 << 20),
        cost_estimate=SMALL,
    )(core, mid, part, other, grad, gain.reshape(1, width), weight, attended)


def first_back_kernel(core, tokens, part, other, mid_grad, gain, grad, gain_sum, shift_sum):
    value = tokens[...].astype(F32)
    center = value - jnp.mean(value, axis=-1, keepdims=True)
    scale = lax.rsqrt(jnp.mean(center * center, axis=-1, keepdims=True) + EPS)
    hat = center * scale
    error = part[...].astype(F32) + other[...].astype(F32)
    scaled = error * gain[...]
    mean = jnp.mean(scaled, axis=-1, keepdims=True)
    dot = jnp.mean(scaled * hat, axis=-1, keepdims=True)
    grad[...] = (mid_grad[...] + (scaled - mean - hat * dot) * scale).astype(BF)

    @pl.when(pl.program_id(0) == 0)
    def _():
        gain_sum[...] = jnp.zeros_like(gain_sum)
        shift_sum[...] = jnp.zeros_like(shift_sum)

    gain_sum[...] += jnp.sum(error * hat, axis=0, keepdims=True)
    shift_sum[...] += jnp.sum(error, axis=0, keepdims=True)


def first_back(core, tokens, part, other, mid_grad, gain):
    rows, width = tokens.shape
    cut = 256
    steps = rows // cut
    own = pl.BlockSpec((cut, width), lambda i, core: (i, 0))
    mine = pl.BlockSpec((cut, width), lambda i, core: (core[0] * steps + i, 0))
    one = pl.BlockSpec((1, width), lambda i, core: (0, 0))
    return pl.pallas_call(
        first_back_kernel,
        grid_spec=pltpu.PrefetchScalarGridSpec(
            num_scalar_prefetch=1,
            grid=(steps,),
            in_specs=[own, mine, own, mine, one],
            out_specs=[own, one, one],
        ),
        out_shape=[
            jax.ShapeDtypeStruct((rows, width), BF),
            jax.ShapeDtypeStruct((1, width), F32),
            jax.ShapeDtypeStruct((1, width), F32),
        ],
        compiler_params=pltpu.CompilerParams(vmem_limit_bytes=44 << 20),
        cost_estimate=SMALL,
    )(core, tokens, part, other, mid_grad, gain.reshape(1, width))


def join_kernel(plane, line, from_a, from_b, far_low, far_high, *wholes):
    turn, at = pl.program_id(0), pl.program_id(1)
    half = pl.num_programs(1) // 2

    def put(source):
        start = 0
        for whole in wholes:
            stop = start + whole.shape[-1]
            whole[0, 0, 0] = source[0, :, start:stop]
            start = stop

    pl.when(turn == 0)(lambda: put(line))
    pl.when(turn == 1)(lambda: put(from_a))
    pl.when(turn == 2)(lambda: put(from_b))
    pl.when((turn == 3) & (at < half))(lambda: put(far_low))
    pl.when((turn == 3) & (at >= half))(lambda: put(far_high))


def join(plane, line, near, far, cuts):
    lines, shard, width = line.shape
    half = lines // 2

    def source(turn_of):
        def at(turn, i, plane):
            return (jnp.where(turn == turn_of, i, jnp.where(turn < turn_of, 0, lines - 1)), 0, 0)

        return pl.BlockSpec((1, shard, width), at)

    def low(turn, i, plane):
        return (jnp.where(turn == 3, jnp.minimum(i, half - 1), 0), 0, 0)

    def high(turn, i, plane):
        return (jnp.where(turn == 3, jnp.maximum(i - half, 0), 0), 0, 0)

    def target(turn, i, plane):
        a, b = plane[0], plane[1]
        return (i, jnp.where(turn >= 2, 1 - b, b), jnp.where(turn % 2 == 1, 1 - a, a), 0, 0)

    wholes = pl.pallas_call(
        join_kernel,
        grid_spec=pltpu.PrefetchScalarGridSpec(
            num_scalar_prefetch=1,
            grid=(4, lines),
            in_specs=[
                source(0),
                source(1),
                source(2),
                pl.BlockSpec((1, shard, width), low),
                pl.BlockSpec((1, shard, width), high),
            ],
            out_specs=[pl.BlockSpec((1, 1, 1, shard, cut), target) for cut in cuts],
        ),
        out_shape=[jax.ShapeDtypeStruct((lines, 2, 2, shard, cut), line.dtype) for cut in cuts],
        compiler_params=pltpu.CompilerParams(vmem_limit_bytes=24 << 20),
        cost_estimate=SMALL,
    )(plane, line, *near, *far)
    return [whole.reshape(lines * 4 * shard, whole.shape[-1]) for whole in wholes]


def weave_kernel(core, mine, theirs, out, *, block):
    own, other = mine[...].astype(F32), theirs[...].astype(F32)
    first = jnp.where(core[0] == 0, own, other)
    second = jnp.where(core[0] == 0, other, own)
    pieces = []
    for start in range(0, first.shape[1], block):
        pieces += [first[:, start : start + block], second[:, start : start + block]]
    out[...] = jnp.concatenate(pieces, axis=1)


def weave(core, mine, theirs, block):
    rows, width = mine.shape
    if rows % 8:
        first = jnp.where(core[0] == 0, mine, theirs).reshape(rows, width // block, 1, block)
        second = jnp.where(core[0] == 0, theirs, mine).reshape(rows, width // block, 1, block)
        return jnp.concatenate([first, second], axis=2).reshape(rows, 2 * width).astype(F32)
    vmem = pl.BlockSpec(memory_space=pltpu.VMEM)
    return pl.pallas_call(
        functools.partial(weave_kernel, block=block),
        in_specs=[pl.BlockSpec(memory_space=pltpu.SMEM), vmem, vmem],
        out_specs=vmem,
        out_shape=jax.ShapeDtypeStruct((rows, 2 * width), F32),
        compiler_params=pltpu.CompilerParams(vmem_limit_bytes=12 << 20),
        cost_estimate=SMALL,
    )(core, mine, theirs)


def make_body(devices):
    chips = devices // 2
    lines = chips // 4

    def place(line, b, a, core):
        return ((line * 2 + b) * 2 + a) * 2 + core

    every = [
        (line, b, a, core)
        for line in range(lines)
        for b in range(2)
        for a in range(2)
        for core in range(2)
    ]
    core_pairs = [(place(*at), place(at[0], at[1], at[2], 1 - at[3])) for at in every]
    a_pairs = [(place(*at), place(at[0], at[1], 1 - at[2], at[3])) for at in every]
    b_pairs = [(place(*at), place(at[0], 1 - at[1], at[2], at[3])) for at in every]
    groups = [
        [place(line, b, a, core) for line in range(lines)]
        for b in range(2)
        for a in range(2)
        for core in range(2)
    ]
    half = lines // 2

    def swap_core(value):
        return lax.ppermute(value, "dev", core_pairs)

    def swap_a(value):
        return lax.ppermute(value, "dev", a_pairs)

    def swap_b(value):
        return lax.ppermute(value, "dev", b_pairs)

    def body(
        tokens,
        lengths,
        out_grad,
        first_gain,
        first_shift,
        query_weight,
        query_bias,
        key_weight,
        value_weight,
        value_bias,
        proj_weight,
        proj_bias,
        mid_gain,
        mid_shift,
        up_weight,
        up_bias,
        down_weight,
        down_bias,
    ):
        position = lax.axis_index("dev")
        core = position % 2
        chip = position // 2
        at_a = chip % 2
        at_b = (chip // 2) % 2
        own_rows, width = tokens.shape
        rows = 2 * own_rows
        shard = query_weight.shape[0]
        side = width // 2
        hidden = up_weight.shape[1]
        block = hidden // devices
        part = block // 2
        spread = block // shard
        length = lax.dynamic_slice(lengths, (chip,), (1,))

        def both(own, other):
            first = jnp.where(core == 0, own, other)
            second = jnp.where(core == 0, other, own)
            return jnp.concatenate([first, second], axis=0)

        def columns(weight, which):
            return lax.dynamic_slice(weight, (0, which * side), (weight.shape[0], side))

        def blocks(weight, which):
            cut = weight.reshape(weight.shape[0], chips, 2, block)
            return lax.dynamic_index_in_dim(cut, which, 2, keepdims=False).reshape(
                weight.shape[0], chips * block
            )

        def after(value, *earlier):
            return lax.optimization_barrier((value, *earlier))[0]

        def gather_line(value):
            return lax.all_gather(value, "dev", axis=0, axis_index_groups=groups)

        def gather_near(line):
            return swap_a(line), swap_b(line)

        def gather_far(near):
            from_a, from_b = near
            return swap_a(from_b[:half]), swap_b(from_a[half:])

        plane = jnp.stack([at_a, at_b]).astype(jnp.int32)

        def ordered(index, own, other):
            return jnp.stack([jnp.where(index == 0, own, other), jnp.where(index == 0, other, own)])

        def gather_plane(value):
            value = ordered(at_a, value, swap_a(value))
            return ordered(at_b, value, swap_b(value))

        def parts_of(whole):
            parts = whole.reshape(lines, 2, 2, whole.shape[0] // chips, whole.shape[1])

            def pick(b, a):
                at = lax.dynamic_index_in_dim(parts, b, 1, keepdims=False)
                return lax.dynamic_index_in_dim(at, a, 1, keepdims=False)

            return pick

        def give_far(pick):
            far = pick(1 - at_b, 1 - at_a)
            return far[:half], far[half:]

        def scatter_far(pick):
            given = give_far(pick)
            return swap_a(given[0]), swap_b(given[1])

        def scatter_add(pick, far):
            far_low, far_high = far
            to_a = pick(at_b, 1 - at_a)
            to_b = pick(1 - at_b, at_a)
            to_a = jnp.concatenate([to_a[:half], to_a[half:] + far_high], axis=0)
            to_b = jnp.concatenate([to_b[:half] + far_low, to_b[half:]], axis=0)
            return to_a, to_b

        def scatter_near(given):
            return swap_a(given[0]), swap_b(given[1])

        def scatter_own(pick, near):
            own = pick(at_b, at_a).astype(F32) + near[0].astype(F32) + near[1].astype(F32)
            return own.astype(BF)

        def scatter_a(parts):
            own = lax.dynamic_index_in_dim(parts, at_a, 1, keepdims=False)
            return own + swap_a(lax.dynamic_index_in_dim(parts, 1 - at_a, 1, keepdims=False))

        def scatter_b(parts):
            own = lax.dynamic_index_in_dim(parts, at_b, 0, keepdims=False)
            return own + swap_b(lax.dynamic_index_in_dim(parts, 1 - at_b, 0, keepdims=False))

        def scatter_line(parts):
            return lax.psum_scatter(
                parts, "dev", scatter_dimension=0, axis_index_groups=groups
            )

        other = 1 - core
        vectors = jnp.stack(
            [first_gain, first_shift, query_bias, value_bias, proj_bias, mid_gain, mid_shift, down_bias],
            axis=1,
        )
        vectors = jnp.concatenate([vectors, up_bias.reshape(shard, spread)], axis=1)
        vectors = jnp.pad(vectors, ((0, 0), (0, VECTORS - vectors.shape[1])))
        own_qkv = jnp.concatenate(
            [columns(query_weight, core), columns(key_weight, core), columns(value_weight, core), vectors, columns(proj_weight, core)],
            axis=1,
        )
        give_qkv = jnp.concatenate(
            [columns(query_weight, other), columns(key_weight, other), columns(value_weight, other), vectors, columns(proj_weight, other)],
            axis=1,
        )
        qkv_shard = both(own_qkv, swap_core(give_qkv))
        all_tokens = both(tokens, swap_core(tokens)).astype(F32)
        tokens, up_weight = lax.optimization_barrier((tokens, up_weight, qkv_shard))[:2]
        rest_shard = both(blocks(up_weight, core), swap_core(blocks(up_weight, other)))
        all_grad = both(out_grad, swap_core(out_grad))
        live = jnp.arange(rows) < length[0]
        grad_low = jnp.where(live[:, None], all_grad, jnp.zeros_like(all_grad))

        def put(whole, block_of, line_at, b, a):
            zero = jnp.int32(0)
            return lax.dynamic_update_slice(
                whole, block_of[:, None, None], (jnp.int32(line_at), b, a, zero, zero)
            )

        qkv_line = gather_line(qkv_shard)
        rest_line = gather_line(rest_shard)
        down_plane = gather_plane(after(down_weight, qkv_shard))
        w_down = gather_line(down_plane).reshape(chips * block, width)
        qkv_near = gather_near(after(qkv_line, down_plane))
        from_a, from_b = qkv_near
        down_b_grad = 0.5 * jnp.sum(grad_low.astype(F32), axis=0)
        from_a, from_b, grad_low, down_b_grad = lax.optimization_barrier((from_a, from_b, grad_low, down_b_grad))
        given_far = (from_b[:half], from_a[half:])
        qkv_far = swap_a(given_far[0]), swap_b(given_far[1])
        rest_near = gather_near(after(rest_line, *given_far))
        w_qkv = jnp.zeros((lines, 2, 2, 2 * shard, 4 * side + VECTORS), BF)
        w_qkv = put(w_qkv, qkv_line, 0, at_b, at_a)
        w_qkv = put(w_qkv, from_a, 0, at_b, 1 - at_a)
        w_qkv = put(w_qkv, from_b, 0, 1 - at_b, at_a)
        w_qkv = put(w_qkv, qkv_far[0], 0, 1 - at_b, 1 - at_a)
        w_qkv = put(w_qkv, qkv_far[1], half, 1 - at_b, 1 - at_a)
        w_qkv = w_qkv.reshape(width, 4 * side + VECTORS)
        table = w_qkv[:, 3 * side : 3 * side + VECTORS].astype(F32).T
        w_proj_side = w_qkv[:, 3 * side + VECTORS :]
        w_qkv = w_qkv[:, : 3 * side]
        gain_one, shift_one, b_query, b_value, b_proj, gain_two, shift_two, b_down = (
            table[i] for i in range(8)
        )
        hidden_bias = table[8 : 8 + spread].reshape(spread, chips, 2, shard)
        hidden_bias = lax.dynamic_index_in_dim(hidden_bias, core, 2, keepdims=False)
        hidden_bias = hidden_bias.transpose(1, 2, 0).reshape(chips * block)

        def rows_of(value, which):
            return lax.dynamic_slice(value, (which * own_rows, 0), (own_rows, value.shape[1]))

        def own_side(vector):
            return lax.dynamic_slice(vector, (core * side,), (side,))

        def normalize(value, gain, shift):
            center = value - jnp.mean(value, axis=-1, keepdims=True)
            spread_of = jnp.mean(center * center, axis=-1, keepdims=True)
            scale = lax.rsqrt(spread_of + EPS)
            hat = center * scale
            return hat * gain + shift, hat, scale

        def normalize_back(grad, hat, scale, gain):
            scaled = grad * gain
            mean = jnp.mean(scaled, axis=-1, keepdims=True)
            dot = jnp.mean(scaled * hat, axis=-1, keepdims=True)
            return (
                (scaled - mean - hat * dot) * scale,
                jnp.sum(grad * hat, axis=0),
                jnp.sum(grad, axis=0),
            )

        normed = normalize(all_tokens, gain_one, shift_one)[0].astype(BF)
        qkv_bias = jnp.concatenate([own_side(b_query), jnp.zeros((side,), F32), own_side(b_value)])
        qkv = (contract(w_qkv[:, : 3 * side], normed, 0, 1) + qkv_bias[:, None]).astype(BF).reshape(3, side, rows)
        attended_own, log_total = attend(length, qkv)
        attended_own, *rest_near = lax.optimization_barrier((attended_own, *rest_near))
        rest_far = gather_far(rest_near)
        attended = after(both(attended_own, swap_core(attended_own)))
        w_proj_other = swap_core(w_proj_side)
        w_proj = jnp.concatenate(
            [
                jnp.where(core == 0, w_proj_side, w_proj_other),
                jnp.where(core == 0, w_proj_other, w_proj_side),
            ],
            axis=1,
        )
        w_proj = after(w_proj)
        mid = all_tokens + contract(attended, w_proj, 0, 0) + b_proj
        mid_normed, mid_hat, mid_scale = normalize(mid, gain_two, shift_two)
        mid_low = mid_normed.astype(BF)
        mid, mid_low, *rest_far = lax.optimization_barrier((mid, mid_low, *rest_far))
        w_up = join(plane, rest_line, rest_near, rest_far, (chips * block,))[0]
        pre_act = contract(mid_low, w_up, 1, 0) + hidden_bias
        below = 0.5 + 0.5 * lax.erf(pre_act * math.sqrt(0.5))
        activ = (pre_act * below).astype(BF)
        slope = (below + pre_act * (jnp.exp(-0.5 * pre_act * pre_act) * (1.0 / math.sqrt(2.0 * math.pi)))).astype(BF)
        activ, slope = lax.optimization_barrier((activ, slope))

        down_grad = contract(activ, grad_low, 0, 0).astype(BF)
        late_line = lax.psum_scatter(
            down_grad.reshape(lines, 2, 2, block, width), "dev", scatter_dimension=0, axis_index_groups=groups
        )
        w_down = after(w_down, down_grad)
        pre_grad = (contract(grad_low, w_down, 1, 1) * slope.astype(F32)).astype(BF)
        mid_part = contract(pre_grad, w_up, 1, 1).astype(BF)
        mid_other = swap_core(mid_part)
        up_grad = contract(after(mid_low, mid_part), pre_grad, 0, 0).astype(BF)
        up_pick = parts_of(up_grad)
        up_give = give_far(up_pick)
        up_far = swap_a(up_give[0]), swap_b(up_give[1])
        up_b_grad = jnp.sum(pre_grad.astype(F32), axis=0)
        mid_other, _, _ = lax.optimization_barrier((mid_other, *up_give))
        mid_grad, attended_grad, proj_grad, *mid_sums = norm_back(
            core.reshape(1).astype(jnp.int32), mid, mid_part, mid_other, grad_low, gain_two, w_proj, attended
        )
        mid_grad, attended_grad, proj_grad, *up_far = lax.optimization_barrier(
            (mid_grad, attended_grad, proj_grad, *up_far)
        )
        gain_two_grad, shift_two_grad, proj_b_grad = (0.5 * item[0] for item in mid_sums)
        up_given = scatter_add(up_pick, up_far)
        up_near = scatter_near(up_given)
        proj_pick = parts_of(proj_grad)
        proj_give = give_far(proj_pick)
        proj_far = swap_a(proj_give[0]), swap_b(proj_give[1])
        proj_far = lax.optimization_barrier((*proj_far, *up_given))[:2]
        proj_given = scatter_add(proj_pick, proj_far)
        proj_near = scatter_near(proj_given)
        attended_grad = after(attended_grad, *proj_given, *up_given)
        qkv_back = attend_back(length, qkv, attended_grad, log_total).reshape(3 * side, rows)
        qkv_grad = contract(normed, qkv_back, 0, 1).astype(BF)
        qkv_grad, *up_near = lax.optimization_barrier((qkv_grad, *up_near))
        qkv_pick = parts_of(qkv_grad)
        qkv_give = give_far(qkv_pick)
        qkv_far = swap_a(qkv_give[0]), swap_b(qkv_give[1])
        came = lax.optimization_barrier((*up_near, *proj_near, *qkv_give))
        up_near, proj_near = came[:2], came[2:4]
        up_own = jnp.concatenate([scatter_own(up_pick, up_near), scatter_own(proj_pick, proj_near)], axis=2)
        up_sum = scatter_line(up_own)
        normed_part = contract(after(qkv_back, up_own), w_qkv[:, : 3 * side], 0, 1).astype(BF)
        normed_other = swap_core(rows_of(normed_part, other))
        normed_part, late_line, *qkv_far = lax.optimization_barrier((normed_part, late_line, *qkv_far))
        qkv_given = scatter_add(qkv_pick, qkv_far)
        qkv_near = scatter_near(qkv_given)
        down_part = product(after(activ, *qkv_given), w_down)
        qkv_b_grad = jnp.sum(after(qkv_back, *qkv_given).astype(F32), axis=1)
        normed_part, *_ = lax.optimization_barrier((normed_part, *qkv_given))
        input_grad, gain_one_grad, shift_one_grad = first_back(
            core.reshape(1).astype(jnp.int32), tokens, normed_part, normed_other, mid_grad, gain_one
        )
        gain_one_grad, shift_one_grad = gain_one_grad[0], shift_one_grad[0]

        def on_side(vector):
            return lax.dynamic_update_slice(jnp.zeros((width,), F32), vector, (core * side,))

        up_rows = up_b_grad.reshape(chips, 1, shard, spread)
        up_rows = lax.dynamic_update_slice(
            jnp.zeros((chips, 2, shard, spread), F32), up_rows, (0, core, 0, 0)
        ).reshape(width, spread)
        sums = jnp.stack(
            [
                gain_one_grad,
                shift_one_grad,
                on_side(qkv_b_grad[:side]),
                on_side(qkv_b_grad[2 * side :]),
                proj_b_grad,
                gain_two_grad,
                shift_two_grad,
                down_b_grad,
            ],
            axis=1,
        )
        sums = jnp.concatenate([sums, up_rows], axis=1)
        sums = jnp.pad(sums, ((0, 0), (0, VECTORS - sums.shape[1]))).astype(BF)
        sums = after(sums, input_grad)
        sums = sums.reshape(lines, 2, 2, 2 * shard, VECTORS)

        def pick(b, a):
            at = lax.dynamic_index_in_dim(sums, b, 1, keepdims=False)
            return lax.dynamic_index_in_dim(at, a, 1, keepdims=False)

        def halves(parts, axis, at):
            own = lax.dynamic_index_in_dim(parts, at, axis, keepdims=False)
            return own, lax.dynamic_index_in_dim(parts, 1 - at, axis, keepdims=False)

        vector_come = swap_a(jnp.stack([pick(at_b, 1 - at_a), pick(1 - at_b, 1 - at_a)]))
        down_other = swap_core(rows_of(down_part, other))
        output = (
            rows_of(mid, core) + rows_of(down_part, core).astype(F32) + down_other.astype(F32) + b_down
        ).astype(BF)
        output, sums, vector_come, late_line, *qkv_near = lax.optimization_barrier(
            (output, sums, vector_come, late_line, *qkv_near)
        )
        vector_near = swap_b(pick(1 - at_b, at_a) + vector_come[1])
        late_keep, late_give = halves(late_line, 1, at_a)
        late_come = swap_a(late_give)
        qkv_own = scatter_own(qkv_pick, qkv_near)
        vector_own = pick(at_b, at_a) + vector_come[0] + vector_near
        own = jnp.concatenate([qkv_own, vector_own], axis=2)
        qkv_sum = scatter_line(own)
        late_keep, late_come, _ = lax.optimization_barrier((late_keep, late_come, own))
        late_keep, late_give = halves(late_keep + late_come, 0, at_b)
        late_sum = late_keep + swap_b(late_give)

        def finish(sum_of, which):
            return lax.dynamic_slice(sum_of, (which * shard, 0), (shard, sum_of.shape[1]))

        def exchange(sum_of):
            mine = finish(sum_of, core)
            theirs = swap_core(finish(sum_of, other))
            left = jnp.where(core == 0, mine, theirs).astype(F32)
            right = jnp.where(core == 0, theirs, mine).astype(F32)
            return left, right

        rest_mine = finish(up_sum, core)
        rest_theirs = swap_core(finish(up_sum, other))
        hidden_own = chips * block
        up_all = weave(core.reshape(1).astype(jnp.int32), rest_mine[:, :hidden_own], rest_theirs[:, :hidden_own], block)
        proj_mine, proj_theirs = rest_mine[:, hidden_own:], rest_theirs[:, hidden_own:]
        proj_all = jnp.concatenate(
            [jnp.where(core == 0, proj_mine, proj_theirs), jnp.where(core == 0, proj_theirs, proj_mine)], axis=1
        ).astype(F32)
        down_sum = late_sum
        qkv_left, qkv_right = exchange(
            lax.optimization_barrier((qkv_sum, up_all, proj_all, down_sum, output))[0]
        )

        def joined(left, right, start):
            return jnp.concatenate([left[:, start : start + side], right[:, start : start + side]], axis=1)

        at_vectors = slice(3 * side, 3 * side + 8 + spread)
        vector_rows = qkv_left[:, at_vectors] + qkv_right[:, at_vectors]
        return (
            output,
            input_grad,
            vector_rows[:, 0],
            vector_rows[:, 1],
            joined(qkv_left, qkv_right, 0),
            vector_rows[:, 2],
            joined(qkv_left, qkv_right, side),
            joined(qkv_left, qkv_right, 2 * side),
            vector_rows[:, 3],
            proj_all,
            vector_rows[:, 4],
            vector_rows[:, 5],
            vector_rows[:, 6],
            up_all,
            vector_rows[:, 8 : 8 + spread].reshape(block),
            down_sum.astype(F32),
            vector_rows[:, 7],
        )

    return body


def solution(mesh):
    matrix, vector = P("dev", None), P("dev")
    return jax.shard_map(
        make_body(mesh.shape["dev"]),
        mesh=mesh,
        in_specs=(
            matrix,
            P(),
            matrix,
            vector,
            vector,
            matrix,
            vector,
            matrix,
            matrix,
            vector,
            matrix,
            vector,
            vector,
            vector,
            matrix,
            vector,
            matrix,
            vector,
        ),
        out_specs=(
            matrix,
            matrix,
            vector,
            vector,
            matrix,
            vector,
            matrix,
            matrix,
            vector,
            matrix,
            vector,
            vector,
            vector,
            matrix,
            vector,
            matrix,
            vector,
        ),
        check_vma=False,
    )
```

```python
import functools
import math

import jax
import jax.numpy as jnp
from jax import lax
from jax.experimental import pallas as pl
from jax.experimental.pallas import tpu as pltpu
from jax.sharding import PartitionSpec as P

HD = 80
EPS = 1e-05
NEG = -1e30
SCALE = HD**-0.5
LOG2E = math.log2(math.e)
BF = jnp.bfloat16
F32 = jnp.float32
VECTORS = 128
PAD = 16
SMALL = pl.CostEstimate(flops=1, bytes_accessed=1, transcendentals=0)


def contract(left, right, left_dim, right_dim):
    return lax.dot_general(
        left, right, (((left_dim,), (right_dim,)), ((), ())), preferred_element_type=F32
    )


def attend_kernel(length, qkv, attended, log_total):
    rows = qkv.shape[2]
    keys = qkv[1].T
    dead = lax.broadcasted_iota(jnp.int32, (rows, 1), 0) >= length[0]
    scores = contract(keys, qkv[0], 1, 0) + jnp.where(dead, NEG, 0.0).astype(F32)
    top = jnp.max(scores, axis=0, keepdims=True)
    weights = jnp.exp2((scores - top) * (SCALE * LOG2E))
    total = jnp.sum(weights, axis=0, keepdims=True)
    probs = (weights * (1.0 / total)).astype(BF)
    attended[...] = contract(qkv[2], probs, 1, 0).astype(BF)
    log_total[0] = top * (SCALE * LOG2E) + jnp.log2(total)


def attend(length, qkv):
    _, width, rows = qkv.shape
    heads = width // HD
    return pl.pallas_call(
        attend_kernel,
        grid=(heads,),
        in_specs=[
            pl.BlockSpec(memory_space=pltpu.SMEM),
            pl.BlockSpec((3, HD, rows), lambda h: (0, h, 0)),
        ],
        out_specs=[
            pl.BlockSpec((HD, rows), lambda h: (h, 0)),
            pl.BlockSpec((1, 1, rows), lambda h: (h, 0, 0)),
        ],
        out_shape=[
            jax.ShapeDtypeStruct((width, rows), BF),
            jax.ShapeDtypeStruct((heads, 1, rows), F32),
        ],
        compiler_params=pltpu.CompilerParams(vmem_limit_bytes=40 << 20),
        cost_estimate=SMALL,
    )(length, qkv)


def term_rows(row, first):
    high = row.astype(BF).astype(F32)
    middle = (row - high).astype(BF).astype(F32)
    at = lax.broadcasted_iota(jnp.int32, (PAD, row.shape[1]), 0)
    terms = jnp.where(at == 1, high, jnp.where(at == 2, middle, jnp.where(at == 3, row - high - middle, 0.0)))
    return jnp.where(at == 0, first, terms).astype(BF)


def attend_back_kernel(length, qkv, out_grad, log_total, grads):
    rows = qkv.shape[2]
    at = lax.broadcasted_iota(jnp.int32, (rows, PAD), 1)
    dead = lax.broadcasted_iota(jnp.int32, (rows, PAD), 0) >= length[0]
    ones = jnp.where((at > 0) & (at < 4), 1.0, 0.0)
    mask = jnp.where((at == 0) & dead, NEG, ones)
    queries, out_part = qkv[0], out_grad[...]
    keys = jnp.concatenate([qkv[1].T, mask.astype(BF)], axis=1)
    query_terms = jnp.concatenate([queries, term_rows(log_total[0] * (-1.0 / (SCALE * LOG2E)), 1.0)], axis=0)
    probs = jnp.exp2(contract(keys, query_terms, 1, 0) * (SCALE * LOG2E))
    prob_grad = contract(qkv[2].T, out_part, 1, 0)
    inner = jnp.sum(probs * prob_grad, axis=0, keepdims=True)
    score_grad = (probs * (prob_grad - inner)).astype(BF)
    grads[0] = (contract(qkv[1], score_grad, 1, 0) * SCALE).astype(BF)
    grads[1] = (contract(score_grad, queries.T, 1, 0) * SCALE).astype(BF).T
    grads[2] = contract(probs.astype(BF), out_part.T, 1, 0).astype(BF).T


def attend_back(length, qkv, out_grad, log_total):
    _, width, rows = qkv.shape
    heads = width // HD
    head = pl.BlockSpec((HD, rows), lambda h: (h, 0))
    triple = pl.BlockSpec((3, HD, rows), lambda h: (0, h, 0))
    return pl.pallas_call(
        attend_back_kernel,
        grid=(heads,),
        in_specs=[
            pl.BlockSpec(memory_space=pltpu.SMEM),
            triple,
            head,
            pl.BlockSpec((1, 1, rows), lambda h: (h, 0, 0)),
        ],
        out_specs=triple,
        out_shape=jax.ShapeDtypeStruct((3, width, rows), BF),
        compiler_params=pltpu.CompilerParams(vmem_limit_bytes=24 << 20),
        cost_estimate=SMALL,
    )(length, qkv, out_grad, log_total)


def product_kernel(left, right, out):
    out[...] = contract(left[...], right[...], 1, 0).astype(BF)


def product(left, right):
    rows, depth = left.shape
    width = right.shape[1]
    return pl.pallas_call(
        product_kernel,
        grid=(width // 256,),
        in_specs=[
            pl.BlockSpec((rows, depth), lambda i: (0, 0), pipeline_mode=pl.Buffered(1)),
            pl.BlockSpec((depth, 256), lambda i: (0, i)),
        ],
        out_specs=pl.BlockSpec((rows, 256), lambda i: (0, i)),
        out_shape=jax.ShapeDtypeStruct((rows, width), BF),
        compiler_params=pltpu.CompilerParams(vmem_limit_bytes=60 << 20),
        cost_estimate=SMALL,
    )(left, right)


def norm_back_kernel(
    core, mid, part, other, grad, gain, heads, attended,
    mid_grad, attended_grad, proj_grad, gain_sum, shift_sum, branch_sum, total, held,
):
    at = pl.program_id(0)
    value = mid[...]
    center = value - jnp.mean(value, axis=-1, keepdims=True)
    scale = lax.rsqrt(jnp.mean(center * center, axis=-1, keepdims=True) + EPS)
    hat = center * scale
    error = part[...].astype(F32) + other[...].astype(F32)
    scaled = error * gain[...]
    mean = jnp.mean(scaled, axis=-1, keepdims=True)
    dot = jnp.mean(scaled * hat, axis=-1, keepdims=True)
    summed = grad[...].astype(F32) + (scaled - mean - hat * dot) * scale
    low = summed.astype(BF)
    mid_grad[...] = summed
    held[...] = low
    attended_grad[...] = contract(heads[...], low, 1, 1).astype(BF)
    side = proj_grad.shape[1]
    columns = held[:, pl.ds(pl.multiple_of(core[0] * side, 128), side)]

    @pl.when(at == 0)
    def _():
        total[...] = jnp.zeros_like(total)
        gain_sum[...] = jnp.zeros_like(gain_sum)
        shift_sum[...] = jnp.zeros_like(shift_sum)
        branch_sum[...] = jnp.zeros_like(branch_sum)

    total[...] += contract(attended[...], columns, 1, 0)
    gain_sum[...] += jnp.sum(error * hat, axis=0, keepdims=True)
    shift_sum[...] += jnp.sum(error, axis=0, keepdims=True)
    branch_sum[...] += jnp.sum(low.astype(F32), axis=0, keepdims=True)

    @pl.when(at == pl.num_programs(0) - 1)
    def _():
        proj_grad[...] = total[...].astype(BF)


def norm_back(core, mid, part, other, grad, gain, weight, attended):
    rows, width = mid.shape
    side = width // 2
    cut = 256
    row = pl.BlockSpec((cut, width), lambda i, core: (i, 0))
    one = pl.BlockSpec((1, width), lambda i, core: (0, 0))
    return pl.pallas_call(
        norm_back_kernel,
        grid_spec=pltpu.PrefetchScalarGridSpec(
            num_scalar_prefetch=1,
            grid=(rows // cut,),
            in_specs=[
                row,
                row,
                row,
                row,
                one,
                pl.BlockSpec((side, width), lambda i, core: (core[0], 0)),
                pl.BlockSpec((width, cut), lambda i, core: (0, i)),
            ],
            out_specs=[
                row,
                pl.BlockSpec((side, cut), lambda i, core: (0, i)),
                pl.BlockSpec((width, side), lambda i, core: (0, 0)),
                one,
                one,
                one,
            ],
            scratch_shapes=[pltpu.VMEM((width, side), F32), pltpu.VMEM((cut, width), BF)],
        ),
        out_shape=[
            jax.ShapeDtypeStruct((rows, width), F32),
            jax.ShapeDtypeStruct((side, rows), BF),
            jax.ShapeDtypeStruct((width, side), BF),
            jax.ShapeDtypeStruct((1, width), F32),
            jax.ShapeDtypeStruct((1, width), F32),
            jax.ShapeDtypeStruct((1, width), F32),
        ],
        compiler_params=pltpu.CompilerParams(vmem_limit_bytes=44 << 20),
        cost_estimate=SMALL,
    )(core, mid, part, other, grad, gain.reshape(1, width), weight, attended)


def first_back_kernel(core, tokens, part, other, mid_grad, gain, grad, gain_sum, shift_sum):
    value = tokens[...].astype(F32)
    center = value - jnp.mean(value, axis=-1, keepdims=True)
    scale = lax.rsqrt(jnp.mean(center * center, axis=-1, keepdims=True) + EPS)
    hat = center * scale
    error = part[...].astype(F32) + other[...].astype(F32)
    scaled = error * gain[...]
    mean = jnp.mean(scaled, axis=-1, keepdims=True)
    dot = jnp.mean(scaled * hat, axis=-1, keepdims=True)
    grad[...] = (mid_grad[...] + (scaled - mean - hat * dot) * scale).astype(BF)

    @pl.when(pl.program_id(0) == 0)
    def _():
        gain_sum[...] = jnp.zeros_like(gain_sum)
        shift_sum[...] = jnp.zeros_like(shift_sum)

    gain_sum[...] += jnp.sum(error * hat, axis=0, keepdims=True)
    shift_sum[...] += jnp.sum(error, axis=0, keepdims=True)


def first_back(core, tokens, part, other, mid_grad, gain):
    rows, width = tokens.shape
    cut = 256
    steps = rows // cut
    own = pl.BlockSpec((cut, width), lambda i, core: (i, 0))
    mine = pl.BlockSpec((cut, width), lambda i, core: (core[0] * steps + i, 0))
    one = pl.BlockSpec((1, width), lambda i, core: (0, 0))
    return pl.pallas_call(
        first_back_kernel,
        grid_spec=pltpu.PrefetchScalarGridSpec(
            num_scalar_prefetch=1,
            grid=(steps,),
            in_specs=[own, mine, own, mine, one],
            out_specs=[own, one, one],
        ),
        out_shape=[
            jax.ShapeDtypeStruct((rows, width), BF),
            jax.ShapeDtypeStruct((1, width), F32),
            jax.ShapeDtypeStruct((1, width), F32),
        ],
        compiler_params=pltpu.CompilerParams(vmem_limit_bytes=44 << 20),
        cost_estimate=SMALL,
    )(core, tokens, part, other, mid_grad, gain.reshape(1, width))


def join_kernel(plane, line, from_a, from_b, far_low, far_high, *wholes):
    turn, at = pl.program_id(0), pl.program_id(1)
    half = pl.num_programs(1) // 2

    def put(source):
        start = 0
        for whole in wholes:
            stop = start + whole.shape[-1]
            whole[0, 0, 0] = source[0, :, start:stop]
            start = stop

    pl.when(turn == 0)(lambda: put(line))
    pl.when(turn == 1)(lambda: put(from_a))
    pl.when(turn == 2)(lambda: put(from_b))
    pl.when((turn == 3) & (at < half))(lambda: put(far_low))
    pl.when((turn == 3) & (at >= half))(lambda: put(far_high))


def join(plane, line, near, far, cuts):
    lines, shard, width = line.shape
    half = lines // 2

    def source(turn_of):
        def at(turn, i, plane):
            return (jnp.where(turn == turn_of, i, jnp.where(turn < turn_of, 0, lines - 1)), 0, 0)

        return pl.BlockSpec((1, shard, width), at)

    def low(turn, i, plane):
        return (jnp.where(turn == 3, jnp.minimum(i, half - 1), 0), 0, 0)

    def high(turn, i, plane):
        return (jnp.where(turn == 3, jnp.maximum(i - half, 0), 0), 0, 0)

    def target(turn, i, plane):
        a, b = plane[0], plane[1]
        return (i, jnp.where(turn >= 2, 1 - b, b), jnp.where(turn % 2 == 1, 1 - a, a), 0, 0)

    wholes = pl.pallas_call(
        join_kernel,
        grid_spec=pltpu.PrefetchScalarGridSpec(
            num_scalar_prefetch=1,
            grid=(4, lines),
            in_specs=[
                source(0),
                source(1),
                source(2),
                pl.BlockSpec((1, shard, width), low),
                pl.BlockSpec((1, shard, width), high),
            ],
            out_specs=[pl.BlockSpec((1, 1, 1, shard, cut), target) for cut in cuts],
        ),
        out_shape=[jax.ShapeDtypeStruct((lines, 2, 2, shard, cut), line.dtype) for cut in cuts],
        compiler_params=pltpu.CompilerParams(vmem_limit_bytes=24 << 20),
        cost_estimate=SMALL,
    )(plane, line, *near, *far)
    return [whole.reshape(lines * 4 * shard, whole.shape[-1]) for whole in wholes]


def unpack_kernel(core, mine, theirs, *outs):
    rows, width = outs[0].shape
    side = width // 2

    def half_rows(ref):
        both = ref[...].astype(F32)
        return jnp.where(core[0] == 0, both[:rows], both[rows:])

    own, other = half_rows(mine), half_rows(theirs)
    first = jnp.where(core[0] == 0, own, other)
    second = jnp.where(core[0] == 0, other, own)
    for at, out in enumerate(outs[:-1]):
        part = slice(at * side, (at + 1) * side)
        out[:, :side] = first[:, part]
        out[:, side:] = second[:, part]
    outs[-1][...] = own[:, (len(outs) - 1) * side :] + other[:, (len(outs) - 1) * side :]


def unpack(core, mine, theirs, width):
    rows = mine.shape[0] // 2
    side = width // 2
    rest = mine.shape[1] - 3 * side
    if rows % 8:
        own, other = (jnp.where(core[0] == 0, item[:rows], item[rows:]).astype(F32) for item in (mine, theirs))
        first, second = jnp.where(core[0] == 0, own, other), jnp.where(core[0] == 0, other, own)
        cuts = [slice(at * side, (at + 1) * side) for at in range(3)]
        joined = [jnp.concatenate([first[:, cut], second[:, cut]], axis=1) for cut in cuts]
        return joined + [own[:, 3 * side :] + other[:, 3 * side :]]
    vmem = pl.BlockSpec(memory_space=pltpu.VMEM)
    return pl.pallas_call(
        unpack_kernel,
        in_specs=[pl.BlockSpec(memory_space=pltpu.SMEM), vmem, vmem],
        out_specs=[vmem] * 4,
        out_shape=[jax.ShapeDtypeStruct((rows, width), F32)] * 3 + [jax.ShapeDtypeStruct((rows, rest), F32)],
        compiler_params=pltpu.CompilerParams(vmem_limit_bytes=60 << 20),
        cost_estimate=SMALL,
    )(core, mine, theirs)


def weave_kernel(core, mine, theirs, out, *, block):
    own, other = mine[...].astype(F32), theirs[...].astype(F32)
    first = jnp.where(core[0] == 0, own, other)
    second = jnp.where(core[0] == 0, other, own)
    pieces = []
    for start in range(0, first.shape[1], block):
        pieces += [first[:, start : start + block], second[:, start : start + block]]
    out[...] = jnp.concatenate(pieces, axis=1)


def weave(core, mine, theirs, block):
    rows, width = mine.shape
    if rows % 8:
        first = jnp.where(core[0] == 0, mine, theirs).reshape(rows, width // block, 1, block)
        second = jnp.where(core[0] == 0, theirs, mine).reshape(rows, width // block, 1, block)
        return jnp.concatenate([first, second], axis=2).reshape(rows, 2 * width).astype(F32)
    vmem = pl.BlockSpec(memory_space=pltpu.VMEM)
    return pl.pallas_call(
        functools.partial(weave_kernel, block=block),
        in_specs=[pl.BlockSpec(memory_space=pltpu.SMEM), vmem, vmem],
        out_specs=vmem,
        out_shape=jax.ShapeDtypeStruct((rows, 2 * width), F32),
        compiler_params=pltpu.CompilerParams(vmem_limit_bytes=12 << 20),
        cost_estimate=SMALL,
    )(core, mine, theirs)


def make_body(devices):
    chips = devices // 2
    lines = chips // 4

    def place(line, b, a, core):
        return ((line * 2 + b) * 2 + a) * 2 + core

    every = [
        (line, b, a, core)
        for line in range(lines)
        for b in range(2)
        for a in range(2)
        for core in range(2)
    ]
    core_pairs = [(place(*at), place(at[0], at[1], at[2], 1 - at[3])) for at in every]
    a_pairs = [(place(*at), place(at[0], at[1], 1 - at[2], at[3])) for at in every]
    b_pairs = [(place(*at), place(at[0], 1 - at[1], at[2], at[3])) for at in every]
    groups = [
        [place(line, b, a, core) for line in range(lines)]
        for b in range(2)
        for a in range(2)
        for core in range(2)
    ]
    half = lines // 2

    def swap_core(value):
        return lax.ppermute(value, "dev", core_pairs)

    def swap_a(value):
        return lax.ppermute(value, "dev", a_pairs)

    def swap_b(value):
        return lax.ppermute(value, "dev", b_pairs)

    def body(
        tokens,
        lengths,
        out_grad,
        first_gain,
        first_shift,
        query_weight,
        query_bias,
        key_weight,
        value_weight,
        value_bias,
        proj_weight,
        proj_bias,
        mid_gain,
        mid_shift,
        up_weight,
        up_bias,
        down_weight,
        down_bias,
    ):
        position = lax.axis_index("dev")
        core = position % 2
        chip = position // 2
        at_a = chip % 2
        at_b = (chip // 2) % 2
        own_rows, width = tokens.shape
        rows = 2 * own_rows
        shard = query_weight.shape[0]
        side = width // 2
        hidden = up_weight.shape[1]
        block = hidden // devices
        part = block // 2
        spread = block // shard
        length = lax.dynamic_slice(lengths, (chip,), (1,))

        def both(own, other):
            first = jnp.where(core == 0, own, other)
            second = jnp.where(core == 0, other, own)
            return jnp.concatenate([first, second], axis=0)

        def columns(weight, which):
            return lax.dynamic_slice(weight, (0, which * side), (weight.shape[0], side))

        def blocks(weight, which):
            cut = weight.reshape(weight.shape[0], chips, 2, block)
            return lax.dynamic_index_in_dim(cut, which, 2, keepdims=False).reshape(
                weight.shape[0], chips * block
            )

        def after(value, *earlier):
            return lax.optimization_barrier((value, *earlier))[0]

        def gather_line(value):
            return lax.all_gather(value, "dev", axis=0, axis_index_groups=groups)

        def gather_near(line):
            return swap_a(line), swap_b(line)

        def gather_far(near):
            from_a, from_b = near
            return swap_a(from_b[:half]), swap_b(from_a[half:])

        plane = jnp.stack([at_a, at_b]).astype(jnp.int32)

        def ordered(index, own, other):
            return jnp.stack([jnp.where(index == 0, own, other), jnp.where(index == 0, other, own)])

        def gather_plane(value):
            value = ordered(at_a, value, swap_a(value))
            return ordered(at_b, value, swap_b(value))

        def parts_of(whole):
            parts = whole.reshape(lines, 2, 2, whole.shape[0] // chips, whole.shape[1])

            def pick(b, a):
                at = lax.dynamic_index_in_dim(parts, b, 1, keepdims=False)
                return lax.dynamic_index_in_dim(at, a, 1, keepdims=False)

            return pick

        def give_far(pick):
            far = pick(1 - at_b, 1 - at_a)
            return far[:half], far[half:]

        def scatter_far(pick):
            given = give_far(pick)
            return swap_a(given[0]), swap_b(given[1])

        def scatter_add(pick, far):
            far_low, far_high = far
            to_a = pick(at_b, 1 - at_a)
            to_b = pick(1 - at_b, at_a)
            to_a = jnp.concatenate([to_a[:half], to_a[half:] + far_high], axis=0)
            to_b = jnp.concatenate([to_b[:half] + far_low, to_b[half:]], axis=0)
            return to_a, to_b

        def scatter_near(given):
            return swap_a(given[0]), swap_b(given[1])

        def scatter_own(pick, near):
            own = pick(at_b, at_a).astype(F32) + near[0].astype(F32) + near[1].astype(F32)
            return own.astype(BF)

        def scatter_a(parts):
            own = lax.dynamic_index_in_dim(parts, at_a, 1, keepdims=False)
            return own + swap_a(lax.dynamic_index_in_dim(parts, 1 - at_a, 1, keepdims=False))

        def scatter_b(parts):
            own = lax.dynamic_index_in_dim(parts, at_b, 0, keepdims=False)
            return own + swap_b(lax.dynamic_index_in_dim(parts, 1 - at_b, 0, keepdims=False))

        def scatter_line(parts):
            return lax.psum_scatter(
                parts, "dev", scatter_dimension=0, axis_index_groups=groups
            )

        other = 1 - core
        vectors = jnp.stack(
            [first_gain, first_shift, query_bias, value_bias, proj_bias, mid_gain, mid_shift, down_bias],
            axis=1,
        )
        vectors = jnp.concatenate([vectors, up_bias.reshape(shard, spread)], axis=1)
        vectors = jnp.pad(vectors, ((0, 0), (0, VECTORS - vectors.shape[1])))
        own_qkv = jnp.concatenate(
            [columns(query_weight, core), columns(key_weight, core), columns(value_weight, core), vectors, columns(proj_weight, core)],
            axis=1,
        )
        give_qkv = jnp.concatenate(
            [columns(query_weight, other), columns(key_weight, other), columns(value_weight, other), vectors, columns(proj_weight, other)],
            axis=1,
        )
        qkv_shard = both(own_qkv, swap_core(give_qkv))
        all_tokens = both(tokens, swap_core(tokens)).astype(F32)
        tokens, up_weight = lax.optimization_barrier((tokens, up_weight, qkv_shard))[:2]
        rest_shard = both(blocks(up_weight, core), swap_core(blocks(up_weight, other)))
        all_grad = both(out_grad, swap_core(out_grad))
        live = jnp.arange(rows) < length[0]
        grad_low = jnp.where(live[:, None], all_grad, jnp.zeros_like(all_grad))

        def put(whole, block_of, line_at, b, a):
            zero = jnp.int32(0)
            return lax.dynamic_update_slice(
                whole, block_of[:, None, None], (jnp.int32(line_at), b, a, zero, zero)
            )

        qkv_line = gather_line(qkv_shard)
        rest_line = gather_line(rest_shard)
        down_plane = gather_plane(after(down_weight, qkv_shard))
        w_down = gather_line(down_plane).reshape(chips * block, width)
        qkv_near = gather_near(after(qkv_line, down_plane))
        from_a, from_b = qkv_near
        down_b_grad = 0.5 * jnp.sum(grad_low.astype(F32), axis=0)
        from_a, from_b, grad_low, down_b_grad = lax.optimization_barrier((from_a, from_b, grad_low, down_b_grad))
        given_far = (from_b[:half], from_a[half:])
        qkv_far = swap_a(given_far[0]), swap_b(given_far[1])
        rest_near = gather_near(after(rest_line, *given_far))
        w_qkv = jnp.zeros((lines, 2, 2, 2 * shard, 4 * side + VECTORS), BF)
        w_qkv = put(w_qkv, qkv_line, 0, at_b, at_a)
        w_qkv = put(w_qkv, from_a, 0, at_b, 1 - at_a)
        w_qkv = put(w_qkv, from_b, 0, 1 - at_b, at_a)
        w_qkv = put(w_qkv, qkv_far[0], 0, 1 - at_b, 1 - at_a)
        w_qkv = put(w_qkv, qkv_far[1], half, 1 - at_b, 1 - at_a)
        w_qkv = w_qkv.reshape(width, 4 * side + VECTORS)
        table = w_qkv[:, 3 * side : 3 * side + VECTORS].astype(F32).T
        w_proj_side = w_qkv[:, 3 * side + VECTORS :]
        w_qkv = w_qkv[:, : 3 * side]
        gain_one, shift_one, b_query, b_value, b_proj, gain_two, shift_two, b_down = (
            table[i] for i in range(8)
        )
        hidden_bias = table[8 : 8 + spread].reshape(spread, chips, 2, shard)
        hidden_bias = lax.dynamic_index_in_dim(hidden_bias, core, 2, keepdims=False)
        hidden_bias = hidden_bias.transpose(1, 2, 0).reshape(chips * block)

        def rows_of(value, which):
            return lax.dynamic_slice(value, (which * own_rows, 0), (own_rows, value.shape[1]))

        def own_side(vector):
            return lax.dynamic_slice(vector, (core * side,), (side,))

        def normalize(value, gain, shift):
            center = value - jnp.mean(value, axis=-1, keepdims=True)
            spread_of = jnp.mean(center * center, axis=-1, keepdims=True)
            scale = lax.rsqrt(spread_of + EPS)
            hat = center * scale
            return hat * gain + shift, hat, scale

        def normalize_back(grad, hat, scale, gain):
            scaled = grad * gain
            mean = jnp.mean(scaled, axis=-1, keepdims=True)
            dot = jnp.mean(scaled * hat, axis=-1, keepdims=True)
            return (
                (scaled - mean - hat * dot) * scale,
                jnp.sum(grad * hat, axis=0),
                jnp.sum(grad, axis=0),
            )

        normed = normalize(all_tokens, gain_one, shift_one)[0].astype(BF)
        qkv_bias = jnp.concatenate([own_side(b_query), jnp.zeros((side,), F32), own_side(b_value)])
        qkv = (contract(w_qkv[:, : 3 * side], normed, 0, 1) + qkv_bias[:, None]).astype(BF).reshape(3, side, rows)
        attended_own, log_total = attend(length, qkv)
        attended_own, *rest_near = lax.optimization_barrier((attended_own, *rest_near))
        rest_far = gather_far(rest_near)
        attended = after(both(attended_own, swap_core(attended_own)))
        w_proj_other = swap_core(w_proj_side)
        w_proj = jnp.concatenate(
            [
                jnp.where(core == 0, w_proj_side, w_proj_other),
                jnp.where(core == 0, w_proj_other, w_proj_side),
            ],
            axis=1,
        )
        w_proj = after(w_proj)
        mid = all_tokens + contract(attended, w_proj, 0, 0) + b_proj
        mid_normed, mid_hat, mid_scale = normalize(mid, gain_two, shift_two)
        mid_low = mid_normed.astype(BF)
        mid, mid_low, *rest_far = lax.optimization_barrier((mid, mid_low, *rest_far))
        w_up = join(plane, rest_line, rest_near, rest_far, (chips * block,))[0]
        pre_act = contract(mid_low, w_up, 1, 0) + hidden_bias
        below = 0.5 + 0.5 * lax.erf(pre_act * math.sqrt(0.5))
        activ = (pre_act * below).astype(BF)
        slope = (below + pre_act * (jnp.exp(-0.5 * pre_act * pre_act) * (1.0 / math.sqrt(2.0 * math.pi)))).astype(BF)
        activ, slope = lax.optimization_barrier((activ, slope))

        down_grad = contract(activ, grad_low, 0, 0).astype(BF)
        late_line = lax.psum_scatter(
            down_grad.reshape(lines, 2, 2, block, width), "dev", scatter_dimension=0, axis_index_groups=groups
        )
        w_down = after(w_down, down_grad)
        pre_grad = (contract(grad_low, w_down, 1, 1) * slope.astype(F32)).astype(BF)
        mid_part = contract(pre_grad, w_up, 1, 1).astype(BF)
        mid_other = swap_core(mid_part)
        up_grad = contract(after(mid_low, mid_part), pre_grad, 0, 0).astype(BF)
        up_pick = parts_of(up_grad)
        up_give = give_far(up_pick)
        up_far = swap_a(up_give[0]), swap_b(up_give[1])
        up_b_grad = jnp.sum(pre_grad.astype(F32), axis=0)
        mid_other, _, _ = lax.optimization_barrier((mid_other, *up_give))
        mid_grad, attended_grad, proj_grad, *mid_sums = norm_back(
            core.reshape(1).astype(jnp.int32), mid, mid_part, mid_other, grad_low, gain_two, w_proj, attended
        )
        mid_grad, attended_grad, proj_grad, *up_far = lax.optimization_barrier(
            (mid_grad, attended_grad, proj_grad, *up_far)
        )
        gain_two_grad, shift_two_grad, proj_b_grad = (0.5 * item[0] for item in mid_sums)
        up_given = scatter_add(up_pick, up_far)
        up_near = scatter_near(up_given)
        proj_pick = parts_of(proj_grad)
        proj_give = give_far(proj_pick)
        proj_far = swap_a(proj_give[0]), swap_b(proj_give[1])
        proj_far = lax.optimization_barrier((*proj_far, *up_given))[:2]
        proj_given = scatter_add(proj_pick, proj_far)
        proj_near = scatter_near(proj_given)
        attended_grad = after(attended_grad, *proj_given, *up_given)
        qkv_back = attend_back(length, qkv, attended_grad, log_total).reshape(3 * side, rows)
        qkv_grad = contract(normed, qkv_back, 0, 1).astype(BF)
        qkv_grad, *up_near = lax.optimization_barrier((qkv_grad, *up_near))
        qkv_pick = parts_of(qkv_grad)
        qkv_give = give_far(qkv_pick)
        qkv_far = swap_a(qkv_give[0]), swap_b(qkv_give[1])
        came = lax.optimization_barrier((*up_near, *proj_near, *qkv_give))
        up_near, proj_near = came[:2], came[2:4]
        up_own = jnp.concatenate([scatter_own(up_pick, up_near), scatter_own(proj_pick, proj_near)], axis=2)
        up_sum = scatter_line(up_own)
        normed_part = contract(after(qkv_back, up_own), w_qkv[:, : 3 * side], 0, 1).astype(BF)
        normed_other = swap_core(rows_of(normed_part, other))
        normed_part, late_line, *qkv_far = lax.optimization_barrier((normed_part, late_line, *qkv_far))
        qkv_given = scatter_add(qkv_pick, qkv_far)
        qkv_near = scatter_near(qkv_given)
        down_part = product(after(activ, *qkv_given), w_down)
        qkv_b_grad = jnp.sum(after(qkv_back, *qkv_given).astype(F32), axis=1)
        normed_part, *_ = lax.optimization_barrier((normed_part, *qkv_given))
        input_grad, gain_one_grad, shift_one_grad = first_back(
            core.reshape(1).astype(jnp.int32), tokens, normed_part, normed_other, mid_grad, gain_one
        )
        gain_one_grad, shift_one_grad = gain_one_grad[0], shift_one_grad[0]

        def on_side(vector):
            return lax.dynamic_update_slice(jnp.zeros((width,), F32), vector, (core * side,))

        up_rows = up_b_grad.reshape(chips, 1, shard, spread)
        up_rows = lax.dynamic_update_slice(
            jnp.zeros((chips, 2, shard, spread), F32), up_rows, (0, core, 0, 0)
        ).reshape(width, spread)
        sums = jnp.stack(
            [
                gain_one_grad,
                shift_one_grad,
                on_side(qkv_b_grad[:side]),
                on_side(qkv_b_grad[2 * side :]),
                proj_b_grad,
                gain_two_grad,
                shift_two_grad,
                down_b_grad,
            ],
            axis=1,
        )
        sums = jnp.concatenate([sums, up_rows], axis=1)
        sums = jnp.pad(sums, ((0, 0), (0, VECTORS - sums.shape[1]))).astype(BF)
        sums = after(sums, input_grad)
        sums = sums.reshape(lines, 2, 2, 2 * shard, VECTORS)

        def pick(b, a):
            at = lax.dynamic_index_in_dim(sums, b, 1, keepdims=False)
            return lax.dynamic_index_in_dim(at, a, 1, keepdims=False)

        def halves(parts, axis, at):
            own = lax.dynamic_index_in_dim(parts, at, axis, keepdims=False)
            return own, lax.dynamic_index_in_dim(parts, 1 - at, axis, keepdims=False)

        vector_come = swap_a(jnp.stack([pick(at_b, 1 - at_a), pick(1 - at_b, 1 - at_a)]))
        down_other = swap_core(rows_of(down_part, other))
        output = (
            rows_of(mid, core) + rows_of(down_part, core).astype(F32) + down_other.astype(F32) + b_down
        ).astype(BF)
        output, sums, vector_come, late_line, *qkv_near = lax.optimization_barrier(
            (output, sums, vector_come, late_line, *qkv_near)
        )
        vector_near = swap_b(pick(1 - at_b, at_a) + vector_come[1])
        late_keep, late_give = halves(late_line, 1, at_a)
        late_come = swap_a(late_give)
        qkv_own = scatter_own(qkv_pick, qkv_near)
        vector_own = pick(at_b, at_a) + vector_come[0] + vector_near
        own = jnp.concatenate([qkv_own, vector_own], axis=2)
        qkv_sum = scatter_line(own)
        late_keep, late_come, _ = lax.optimization_barrier((late_keep, late_come, own))
        late_keep, late_give = halves(late_keep + late_come, 0, at_b)
        late_sum = late_keep + swap_b(late_give)

        def finish(sum_of, which):
            return lax.dynamic_slice(sum_of, (which * shard, 0), (shard, sum_of.shape[1]))

        rest_mine = finish(up_sum, core)
        rest_theirs = swap_core(finish(up_sum, other))
        hidden_own = chips * block
        up_all = weave(core.reshape(1).astype(jnp.int32), rest_mine[:, :hidden_own], rest_theirs[:, :hidden_own], block)
        proj_mine, proj_theirs = rest_mine[:, hidden_own:], rest_theirs[:, hidden_own:]
        proj_all = jnp.concatenate(
            [jnp.where(core == 0, proj_mine, proj_theirs), jnp.where(core == 0, proj_theirs, proj_mine)], axis=1
        ).astype(F32)
        down_sum = late_sum
        qkv_sum = lax.optimization_barrier((qkv_sum, up_all, proj_all, down_sum, output))[0]
        query_all, key_all, value_all, vector_rows = unpack(
            core.reshape(1).astype(jnp.int32), qkv_sum, swap_core(qkv_sum), width
        )
        return (
            output,
            input_grad,
            vector_rows[:, 0],
            vector_rows[:, 1],
            query_all,
            vector_rows[:, 2],
            key_all,
            value_all,
            vector_rows[:, 3],
            proj_all,
            vector_rows[:, 4],
            vector_rows[:, 5],
            vector_rows[:, 6],
            up_all,
            vector_rows[:, 8 : 8 + spread].reshape(block),
            down_sum.astype(F32),
            vector_rows[:, 7],
        )

    return body


def solution(mesh):
    matrix, vector = P("dev", None), P("dev")
    return jax.shard_map(
        make_body(mesh.shape["dev"]),
        mesh=mesh,
        in_specs=(
            matrix,
            P(),
            matrix,
            vector,
            vector,
            matrix,
            vector,
            matrix,
            matrix,
            vector,
            matrix,
            vector,
            vector,
            vector,
            matrix,
            vector,
            matrix,
            vector,
        ),
        out_specs=(
            matrix,
            matrix,
            vector,
            vector,
            matrix,
            vector,
            matrix,
            matrix,
            vector,
            matrix,
            vector,
            vector,
            vector,
            matrix,
            vector,
            matrix,
            vector,
        ),
        check_vma=False,
    )
```

```python
import functools
import math

import jax
import jax.numpy as jnp
from jax import lax
from jax.experimental import pallas as pl
from jax.experimental.pallas import tpu as pltpu
from jax.sharding import PartitionSpec as P

HD = 80
EPS = 1e-05
NEG = -1e30
SCALE = HD**-0.5
LOG2E = math.log2(math.e)
BF = jnp.bfloat16
F32 = jnp.float32
VECTORS = 128
PAD = 16
SMALL = pl.CostEstimate(flops=1, bytes_accessed=1, transcendentals=0)


def contract(left, right, left_dim, right_dim):
    return lax.dot_general(
        left, right, (((left_dim,), (right_dim,)), ((), ())), preferred_element_type=F32
    )


def attend_kernel(length, qkv, attended, log_total):
    rows = qkv.shape[2]
    keys = qkv[1].T
    dead = lax.broadcasted_iota(jnp.int32, (rows, 1), 0) >= length[0]
    scores = contract(keys, qkv[0], 1, 0) + jnp.where(dead, NEG, 0.0).astype(F32)
    top = jnp.max(scores, axis=0, keepdims=True)
    weights = jnp.exp2((scores - top) * (SCALE * LOG2E))
    total = jnp.sum(weights, axis=0, keepdims=True)
    probs = (weights * (1.0 / total)).astype(BF)
    attended[...] = contract(qkv[2], probs, 1, 0).astype(BF)
    log_total[0] = top * (SCALE * LOG2E) + jnp.log2(total)


def attend(length, qkv):
    _, width, rows = qkv.shape
    heads = width // HD
    return pl.pallas_call(
        attend_kernel,
        grid=(heads,),
        in_specs=[
            pl.BlockSpec(memory_space=pltpu.SMEM),
            pl.BlockSpec((3, HD, rows), lambda h: (0, h, 0)),
        ],
        out_specs=[
            pl.BlockSpec((HD, rows), lambda h: (h, 0)),
            pl.BlockSpec((1, 1, rows), lambda h: (h, 0, 0)),
        ],
        out_shape=[
            jax.ShapeDtypeStruct((width, rows), BF),
            jax.ShapeDtypeStruct((heads, 1, rows), F32),
        ],
        compiler_params=pltpu.CompilerParams(vmem_limit_bytes=40 << 20),
        cost_estimate=SMALL,
    )(length, qkv)


def term_rows(row, first):
    high = row.astype(BF).astype(F32)
    middle = (row - high).astype(BF).astype(F32)
    at = lax.broadcasted_iota(jnp.int32, (PAD, row.shape[1]), 0)
    terms = jnp.where(at == 1, high, jnp.where(at == 2, middle, jnp.where(at == 3, row - high - middle, 0.0)))
    return jnp.where(at == 0, first, terms).astype(BF)


def attend_back_kernel(length, qkv, out_grad, log_total, grads):
    rows = qkv.shape[2]
    at = lax.broadcasted_iota(jnp.int32, (rows, PAD), 1)
    dead = lax.broadcasted_iota(jnp.int32, (rows, PAD), 0) >= length[0]
    ones = jnp.where((at > 0) & (at < 4), 1.0, 0.0)
    mask = jnp.where((at == 0) & dead, NEG, ones)
    queries, out_part = qkv[0], out_grad[...]
    keys = jnp.concatenate([qkv[1].T, mask.astype(BF)], axis=1)
    query_terms = jnp.concatenate([queries, term_rows(log_total[0] * (-1.0 / (SCALE * LOG2E)), 1.0)], axis=0)
    probs = jnp.exp2(contract(keys, query_terms, 1, 0) * (SCALE * LOG2E))
    prob_grad = contract(qkv[2].T, out_part, 1, 0)
    inner = jnp.sum(probs * prob_grad, axis=0, keepdims=True)
    score_grad = (probs * (prob_grad - inner)).astype(BF)
    grads[0] = (contract(qkv[1], score_grad, 1, 0) * SCALE).astype(BF)
    grads[1] = (contract(score_grad, queries.T, 1, 0) * SCALE).astype(BF).T
    grads[2] = contract(probs.astype(BF), out_part.T, 1, 0).astype(BF).T


def attend_back(length, qkv, out_grad, log_total):
    _, width, rows = qkv.shape
    heads = width // HD
    head = pl.BlockSpec((HD, rows), lambda h: (h, 0))
    triple = pl.BlockSpec((3, HD, rows), lambda h: (0, h, 0))
    return pl.pallas_call(
        attend_back_kernel,
        grid=(heads,),
        in_specs=[
            pl.BlockSpec(memory_space=pltpu.SMEM),
            triple,
            head,
            pl.BlockSpec((1, 1, rows), lambda h: (h, 0, 0)),
        ],
        out_specs=triple,
        out_shape=jax.ShapeDtypeStruct((3, width, rows), BF),
        compiler_params=pltpu.CompilerParams(vmem_limit_bytes=24 << 20),
        cost_estimate=SMALL,
    )(length, qkv, out_grad, log_total)


def product_kernel(left, right, out):
    out[...] = contract(left[...], right[...], 1, 0).astype(BF)


def product(left, right):
    rows, depth = left.shape
    width = right.shape[1]
    return pl.pallas_call(
        product_kernel,
        grid=(width // 256,),
        in_specs=[
            pl.BlockSpec((rows, depth), lambda i: (0, 0), pipeline_mode=pl.Buffered(1)),
            pl.BlockSpec((depth, 256), lambda i: (0, i)),
        ],
        out_specs=pl.BlockSpec((rows, 256), lambda i: (0, i)),
        out_shape=jax.ShapeDtypeStruct((rows, width), BF),
        compiler_params=pltpu.CompilerParams(vmem_limit_bytes=60 << 20),
        cost_estimate=SMALL,
    )(left, right)


def norm_back_kernel(
    core, mid, part, other, grad, gain, heads, attended,
    mid_grad, attended_grad, proj_grad, gain_sum, shift_sum, branch_sum, total, held,
):
    at = pl.program_id(0)
    value = mid[...]
    center = value - jnp.mean(value, axis=-1, keepdims=True)
    scale = lax.rsqrt(jnp.mean(center * center, axis=-1, keepdims=True) + EPS)
    hat = center * scale
    error = part[...].astype(F32) + other[...].astype(F32)
    scaled = error * gain[...]
    mean = jnp.mean(scaled, axis=-1, keepdims=True)
    dot = jnp.mean(scaled * hat, axis=-1, keepdims=True)
    summed = grad[...].astype(F32) + (scaled - mean - hat * dot) * scale
    low = summed.astype(BF)
    mid_grad[...] = summed
    held[...] = low
    attended_grad[...] = contract(heads[...], low, 1, 1).astype(BF)
    side = proj_grad.shape[1]
    columns = held[:, pl.ds(pl.multiple_of(core[0] * side, 128), side)]

    @pl.when(at == 0)
    def _():
        total[...] = jnp.zeros_like(total)
        gain_sum[...] = jnp.zeros_like(gain_sum)
        shift_sum[...] = jnp.zeros_like(shift_sum)
        branch_sum[...] = jnp.zeros_like(branch_sum)

    total[...] += contract(attended[...], columns, 1, 0)
    gain_sum[...] += jnp.sum(error * hat, axis=0, keepdims=True)
    shift_sum[...] += jnp.sum(error, axis=0, keepdims=True)
    branch_sum[...] += jnp.sum(low.astype(F32), axis=0, keepdims=True)

    @pl.when(at == pl.num_programs(0) - 1)
    def _():
        proj_grad[...] = total[...].astype(BF)


def norm_back(core, mid, part, other, grad, gain, weight, attended):
    rows, width = mid.shape
    side = width // 2
    cut = 256
    row = pl.BlockSpec((cut, width), lambda i, core: (i, 0))
    one = pl.BlockSpec((1, width), lambda i, core: (0, 0))
    return pl.pallas_call(
        norm_back_kernel,
        grid_spec=pltpu.PrefetchScalarGridSpec(
            num_scalar_prefetch=1,
            grid=(rows // cut,),
            in_specs=[
                row,
                row,
                row,
                row,
                one,
                pl.BlockSpec((side, width), lambda i, core: (core[0], 0)),
                pl.BlockSpec((width, cut), lambda i, core: (0, i)),
            ],
            out_specs=[
                row,
                pl.BlockSpec((side, cut), lambda i, core: (0, i)),
                pl.BlockSpec((width, side), lambda i, core: (0, 0)),
                one,
                one,
                one,
            ],
            scratch_shapes=[pltpu.VMEM((width, side), F32), pltpu.VMEM((cut, width), BF)],
        ),
        out_shape=[
            jax.ShapeDtypeStruct((rows, width), F32),
            jax.ShapeDtypeStruct((side, rows), BF),
            jax.ShapeDtypeStruct((width, side), BF),
            jax.ShapeDtypeStruct((1, width), F32),
            jax.ShapeDtypeStruct((1, width), F32),
            jax.ShapeDtypeStruct((1, width), F32),
        ],
        compiler_params=pltpu.CompilerParams(vmem_limit_bytes=44 << 20),
        cost_estimate=SMALL,
    )(core, mid, part, other, grad, gain.reshape(1, width), weight, attended)


def first_back_kernel(core, tokens, part, other, mid_grad, gain, grad, gain_sum, shift_sum):
    value = tokens[...].astype(F32)
    center = value - jnp.mean(value, axis=-1, keepdims=True)
    scale = lax.rsqrt(jnp.mean(center * center, axis=-1, keepdims=True) + EPS)
    hat = center * scale
    error = part[...].astype(F32) + other[...].astype(F32)
    scaled = error * gain[...]
    mean = jnp.mean(scaled, axis=-1, keepdims=True)
    dot = jnp.mean(scaled * hat, axis=-1, keepdims=True)
    grad[...] = (mid_grad[...] + (scaled - mean - hat * dot) * scale).astype(BF)

    @pl.when(pl.program_id(0) == 0)
    def _():
        gain_sum[...] = jnp.zeros_like(gain_sum)
        shift_sum[...] = jnp.zeros_like(shift_sum)

    gain_sum[...] += jnp.sum(error * hat, axis=0, keepdims=True)
    shift_sum[...] += jnp.sum(error, axis=0, keepdims=True)


def first_back(core, tokens, part, other, mid_grad, gain):
    rows, width = tokens.shape
    cut = 256
    steps = rows // cut
    own = pl.BlockSpec((cut, width), lambda i, core: (i, 0))
    mine = pl.BlockSpec((cut, width), lambda i, core: (core[0] * steps + i, 0))
    one = pl.BlockSpec((1, width), lambda i, core: (0, 0))
    return pl.pallas_call(
        first_back_kernel,
        grid_spec=pltpu.PrefetchScalarGridSpec(
            num_scalar_prefetch=1,
            grid=(steps,),
            in_specs=[own, mine, own, mine, one],
            out_specs=[own, one, one],
        ),
        out_shape=[
            jax.ShapeDtypeStruct((rows, width), BF),
            jax.ShapeDtypeStruct((1, width), F32),
            jax.ShapeDtypeStruct((1, width), F32),
        ],
        compiler_params=pltpu.CompilerParams(vmem_limit_bytes=44 << 20),
        cost_estimate=SMALL,
    )(core, tokens, part, other, mid_grad, gain.reshape(1, width))


def join_kernel(plane, line, from_a, from_b, far_low, far_high, *wholes):
    turn, at = pl.program_id(0), pl.program_id(1)
    half = pl.num_programs(1) // 2

    def put(source):
        start = 0
        for whole in wholes:
            stop = start + whole.shape[-1]
            whole[0, 0, 0] = source[0, :, start:stop]
            start = stop

    pl.when(turn == 0)(lambda: put(line))
    pl.when(turn == 1)(lambda: put(from_a))
    pl.when(turn == 2)(lambda: put(from_b))
    pl.when((turn == 3) & (at < half))(lambda: put(far_low))
    pl.when((turn == 3) & (at >= half))(lambda: put(far_high))


def join(plane, line, near, far, cuts):
    lines, shard, width = line.shape
    half = lines // 2

    def source(turn_of):
        def at(turn, i, plane):
            return (jnp.where(turn == turn_of, i, jnp.where(turn < turn_of, 0, lines - 1)), 0, 0)

        return pl.BlockSpec((1, shard, width), at)

    def low(turn, i, plane):
        return (jnp.where(turn == 3, jnp.minimum(i, half - 1), 0), 0, 0)

    def high(turn, i, plane):
        return (jnp.where(turn == 3, jnp.maximum(i - half, 0), 0), 0, 0)

    def target(turn, i, plane):
        a, b = plane[0], plane[1]
        return (i, jnp.where(turn >= 2, 1 - b, b), jnp.where(turn % 2 == 1, 1 - a, a), 0, 0)

    wholes = pl.pallas_call(
        join_kernel,
        grid_spec=pltpu.PrefetchScalarGridSpec(
            num_scalar_prefetch=1,
            grid=(4, lines),
            in_specs=[
                source(0),
                source(1),
                source(2),
                pl.BlockSpec((1, shard, width), low),
                pl.BlockSpec((1, shard, width), high),
            ],
            out_specs=[pl.BlockSpec((1, 1, 1, shard, cut), target) for cut in cuts],
        ),
        out_shape=[jax.ShapeDtypeStruct((lines, 2, 2, shard, cut), line.dtype) for cut in cuts],
        compiler_params=pltpu.CompilerParams(vmem_limit_bytes=24 << 20),
        cost_estimate=SMALL,
    )(plane, line, *near, *far)
    return [whole.reshape(lines * 4 * shard, whole.shape[-1]) for whole in wholes]


def unpack_kernel(core, mine, theirs, *outs):
    rows, width = outs[0].shape
    side = width // 2

    def half_rows(ref):
        both = ref[...].astype(F32)
        return jnp.where(core[0] == 0, both[:rows], both[rows:])

    own, other = half_rows(mine), half_rows(theirs)
    first = jnp.where(core[0] == 0, own, other)
    second = jnp.where(core[0] == 0, other, own)
    for at, out in enumerate(outs[:-1]):
        part = slice(at * side, (at + 1) * side)
        out[:, :side] = first[:, part]
        out[:, side:] = second[:, part]
    outs[-1][...] = own[:, (len(outs) - 1) * side :] + other[:, (len(outs) - 1) * side :]


def unpack(core, mine, theirs, width):
    rows = mine.shape[0] // 2
    side = width // 2
    rest = mine.shape[1] - 3 * side
    if rows % 8:
        own, other = (jnp.where(core[0] == 0, item[:rows], item[rows:]).astype(F32) for item in (mine, theirs))
        first, second = jnp.where(core[0] == 0, own, other), jnp.where(core[0] == 0, other, own)
        cuts = [slice(at * side, (at + 1) * side) for at in range(3)]
        joined = [jnp.concatenate([first[:, cut], second[:, cut]], axis=1) for cut in cuts]
        return joined + [own[:, 3 * side :] + other[:, 3 * side :]]
    vmem = pl.BlockSpec(memory_space=pltpu.VMEM)
    return pl.pallas_call(
        unpack_kernel,
        in_specs=[pl.BlockSpec(memory_space=pltpu.SMEM), vmem, vmem],
        out_specs=[vmem] * 4,
        out_shape=[jax.ShapeDtypeStruct((rows, width), F32)] * 3 + [jax.ShapeDtypeStruct((rows, rest), F32)],
        compiler_params=pltpu.CompilerParams(vmem_limit_bytes=60 << 20),
        cost_estimate=SMALL,
    )(core, mine, theirs)


def weave_kernel(core, mine, theirs, out, *, block):
    own, other = mine[...].astype(F32), theirs[...].astype(F32)
    first = jnp.where(core[0] == 0, own, other)
    second = jnp.where(core[0] == 0, other, own)
    pieces = []
    for start in range(0, first.shape[1], block):
        pieces += [first[:, start : start + block], second[:, start : start + block]]
    out[...] = jnp.concatenate(pieces, axis=1)


def weave(core, mine, theirs, block):
    rows, width = mine.shape
    if rows % 8:
        first = jnp.where(core[0] == 0, mine, theirs).reshape(rows, width // block, 1, block)
        second = jnp.where(core[0] == 0, theirs, mine).reshape(rows, width // block, 1, block)
        return jnp.concatenate([first, second], axis=2).reshape(rows, 2 * width).astype(F32)
    vmem = pl.BlockSpec(memory_space=pltpu.VMEM)
    return pl.pallas_call(
        functools.partial(weave_kernel, block=block),
        in_specs=[pl.BlockSpec(memory_space=pltpu.SMEM), vmem, vmem],
        out_specs=vmem,
        out_shape=jax.ShapeDtypeStruct((rows, 2 * width), F32),
        compiler_params=pltpu.CompilerParams(vmem_limit_bytes=12 << 20),
        cost_estimate=SMALL,
    )(core, mine, theirs)


def make_body(devices):
    chips = devices // 2
    lines = chips // 4

    def place(line, b, a, core):
        return ((line * 2 + b) * 2 + a) * 2 + core

    every = [
        (line, b, a, core)
        for line in range(lines)
        for b in range(2)
        for a in range(2)
        for core in range(2)
    ]
    core_pairs = [(place(*at), place(at[0], at[1], at[2], 1 - at[3])) for at in every]
    a_pairs = [(place(*at), place(at[0], at[1], 1 - at[2], at[3])) for at in every]
    b_pairs = [(place(*at), place(at[0], 1 - at[1], at[2], at[3])) for at in every]
    groups = [
        [place(line, b, a, core) for line in range(lines)]
        for b in range(2)
        for a in range(2)
        for core in range(2)
    ]
    half = lines // 2

    def swap_core(value):
        return lax.ppermute(value, "dev", core_pairs)

    def swap_a(value):
        return lax.ppermute(value, "dev", a_pairs)

    def swap_b(value):
        return lax.ppermute(value, "dev", b_pairs)

    def body(
        tokens,
        lengths,
        out_grad,
        first_gain,
        first_shift,
        query_weight,
        query_bias,
        key_weight,
        value_weight,
        value_bias,
        proj_weight,
        proj_bias,
        mid_gain,
        mid_shift,
        up_weight,
        up_bias,
        down_weight,
        down_bias,
    ):
        position = lax.axis_index("dev")
        core = position % 2
        chip = position // 2
        at_a = chip % 2
        at_b = (chip // 2) % 2
        own_rows, width = tokens.shape
        rows = 2 * own_rows
        shard = query_weight.shape[0]
        side = width // 2
        hidden = up_weight.shape[1]
        block = hidden // devices
        part = block // 2
        spread = block // shard
        length = lax.dynamic_slice(lengths, (chip,), (1,))

        def both(own, other):
            first = jnp.where(core == 0, own, other)
            second = jnp.where(core == 0, other, own)
            return jnp.concatenate([first, second], axis=0)

        def columns(weight, which):
            return lax.dynamic_slice(weight, (0, which * side), (weight.shape[0], side))

        def blocks(weight, which):
            cut = weight.reshape(weight.shape[0], chips, 2, block)
            return lax.dynamic_index_in_dim(cut, which, 2, keepdims=False).reshape(
                weight.shape[0], chips * block
            )

        def after(value, *earlier):
            return lax.optimization_barrier((value, *earlier))[0]

        def gather_line(value):
            return lax.all_gather(value, "dev", axis=0, axis_index_groups=groups)

        def gather_near(line):
            return swap_a(line), swap_b(line)

        def gather_far(near):
            from_a, from_b = near
            return swap_a(from_b[:half]), swap_b(from_a[half:])

        plane = jnp.stack([at_a, at_b]).astype(jnp.int32)

        def ordered(index, own, other):
            return jnp.stack([jnp.where(index == 0, own, other), jnp.where(index == 0, other, own)])

        def gather_plane(value):
            value = ordered(at_a, value, swap_a(value))
            return ordered(at_b, value, swap_b(value))

        def parts_of(whole):
            parts = whole.reshape(lines, 2, 2, whole.shape[0] // chips, whole.shape[1])

            def pick(b, a):
                at = lax.dynamic_index_in_dim(parts, b, 1, keepdims=False)
                return lax.dynamic_index_in_dim(at, a, 1, keepdims=False)

            return pick

        def give_far(pick):
            far = pick(1 - at_b, 1 - at_a)
            return far[:half], far[half:]

        def scatter_far(pick):
            given = give_far(pick)
            return swap_a(given[0]), swap_b(given[1])

        def scatter_add(pick, far):
            far_low, far_high = far
            to_a = pick(at_b, 1 - at_a)
            to_b = pick(1 - at_b, at_a)
            to_a = jnp.concatenate([to_a[:half], to_a[half:] + far_high], axis=0)
            to_b = jnp.concatenate([to_b[:half] + far_low, to_b[half:]], axis=0)
            return to_a, to_b

        def scatter_near(given):
            return swap_a(given[0]), swap_b(given[1])

        def scatter_own(pick, near):
            own = pick(at_b, at_a).astype(F32) + near[0].astype(F32) + near[1].astype(F32)
            return own.astype(BF)

        def scatter_a(parts):
            own = lax.dynamic_index_in_dim(parts, at_a, 1, keepdims=False)
            return own + swap_a(lax.dynamic_index_in_dim(parts, 1 - at_a, 1, keepdims=False))

        def scatter_b(parts):
            own = lax.dynamic_index_in_dim(parts, at_b, 0, keepdims=False)
            return own + swap_b(lax.dynamic_index_in_dim(parts, 1 - at_b, 0, keepdims=False))

        def scatter_line(parts):
            return lax.psum_scatter(
                parts, "dev", scatter_dimension=0, axis_index_groups=groups
            )

        other = 1 - core
        vectors = jnp.stack(
            [first_gain, first_shift, query_bias, value_bias, proj_bias, mid_gain, mid_shift, down_bias],
            axis=1,
        )
        vectors = jnp.concatenate([vectors, up_bias.reshape(shard, spread)], axis=1)
        vectors = jnp.pad(vectors, ((0, 0), (0, VECTORS - vectors.shape[1])))
        own_qkv = jnp.concatenate(
            [columns(query_weight, core), columns(key_weight, core), columns(value_weight, core), vectors, columns(proj_weight, core)],
            axis=1,
        )
        give_qkv = jnp.concatenate(
            [columns(query_weight, other), columns(key_weight, other), columns(value_weight, other), vectors, columns(proj_weight, other)],
            axis=1,
        )
        qkv_shard = both(own_qkv, swap_core(give_qkv))
        all_tokens = both(tokens, swap_core(tokens)).astype(F32)
        tokens, up_weight = lax.optimization_barrier((tokens, up_weight, qkv_shard))[:2]
        rest_shard = both(blocks(up_weight, core), swap_core(blocks(up_weight, other)))
        all_grad = both(out_grad, swap_core(out_grad))
        live = jnp.arange(rows) < length[0]
        grad_low = jnp.where(live[:, None], all_grad, jnp.zeros_like(all_grad))

        def put(whole, block_of, line_at, b, a):
            zero = jnp.int32(0)
            return lax.dynamic_update_slice(
                whole, block_of[:, None, None], (jnp.int32(line_at), b, a, zero, zero)
            )

        qkv_line = gather_line(qkv_shard)
        rest_line = gather_line(rest_shard)
        down_plane = gather_plane(after(down_weight, qkv_shard))
        w_down = gather_line(down_plane).reshape(chips * block, width)
        qkv_near = gather_near(after(qkv_line, down_plane))
        from_a, from_b = qkv_near
        down_b_grad = 0.5 * jnp.sum(grad_low.astype(F32), axis=0)
        from_a, from_b, grad_low, down_b_grad = lax.optimization_barrier((from_a, from_b, grad_low, down_b_grad))
        given_far = (from_b[:half], from_a[half:])
        qkv_far = swap_a(given_far[0]), swap_b(given_far[1])
        rest_near = gather_near(after(rest_line, *given_far))
        w_qkv = jnp.zeros((lines, 2, 2, 2 * shard, 4 * side + VECTORS), BF)
        w_qkv = put(w_qkv, qkv_line, 0, at_b, at_a)
        w_qkv = put(w_qkv, from_a, 0, at_b, 1 - at_a)
        w_qkv = put(w_qkv, from_b, 0, 1 - at_b, at_a)
        w_qkv = put(w_qkv, qkv_far[0], 0, 1 - at_b, 1 - at_a)
        w_qkv = put(w_qkv, qkv_far[1], half, 1 - at_b, 1 - at_a)
        w_qkv = w_qkv.reshape(width, 4 * side + VECTORS)
        table = w_qkv[:, 3 * side : 3 * side + VECTORS].astype(F32).T
        w_proj_side = w_qkv[:, 3 * side + VECTORS :]
        w_qkv = w_qkv[:, : 3 * side]
        gain_one, shift_one, b_query, b_value, b_proj, gain_two, shift_two, b_down = (
            table[i] for i in range(8)
        )
        hidden_bias = table[8 : 8 + spread].reshape(spread, chips, 2, shard)
        hidden_bias = lax.dynamic_index_in_dim(hidden_bias, core, 2, keepdims=False)
        hidden_bias = hidden_bias.transpose(1, 2, 0).reshape(chips * block)

        def rows_of(value, which):
            return lax.dynamic_slice(value, (which * own_rows, 0), (own_rows, value.shape[1]))

        def own_side(vector):
            return lax.dynamic_slice(vector, (core * side,), (side,))

        def normalize(value, gain, shift):
            center = value - jnp.mean(value, axis=-1, keepdims=True)
            spread_of = jnp.mean(center * center, axis=-1, keepdims=True)
            scale = lax.rsqrt(spread_of + EPS)
            hat = center * scale
            return hat * gain + shift, hat, scale

        def normalize_back(grad, hat, scale, gain):
            scaled = grad * gain
            mean = jnp.mean(scaled, axis=-1, keepdims=True)
            dot = jnp.mean(scaled * hat, axis=-1, keepdims=True)
            return (
                (scaled - mean - hat * dot) * scale,
                jnp.sum(grad * hat, axis=0),
                jnp.sum(grad, axis=0),
            )

        normed = normalize(all_tokens, gain_one, shift_one)[0].astype(BF)
        qkv_bias = jnp.concatenate([own_side(b_query), jnp.zeros((side,), F32), own_side(b_value)])
        qkv = (contract(w_qkv[:, : 3 * side], normed, 0, 1) + qkv_bias[:, None]).astype(BF).reshape(3, side, rows)
        attended_own, log_total = attend(length, qkv)
        attended_own, *rest_near = lax.optimization_barrier((attended_own, *rest_near))
        rest_far = gather_far(rest_near)
        attended = after(both(attended_own, swap_core(attended_own)))
        w_proj_other = swap_core(w_proj_side)
        w_proj = jnp.concatenate(
            [
                jnp.where(core == 0, w_proj_side, w_proj_other),
                jnp.where(core == 0, w_proj_other, w_proj_side),
            ],
            axis=1,
        )
        w_proj = after(w_proj)
        mid = all_tokens + contract(attended, w_proj, 0, 0) + b_proj
        mid_normed, mid_hat, mid_scale = normalize(mid, gain_two, shift_two)
        mid_low = mid_normed.astype(BF)
        mid, mid_low, *rest_far = lax.optimization_barrier((mid, mid_low, *rest_far))
        w_up = join(plane, rest_line, rest_near, rest_far, (chips * block,))[0]
        pre_act = contract(mid_low, w_up, 1, 0) + hidden_bias
        below = 0.5 + 0.5 * lax.erf(pre_act * math.sqrt(0.5))
        activ = (pre_act * below).astype(BF)
        slope = (below + pre_act * (jnp.exp(-0.5 * pre_act * pre_act) * (1.0 / math.sqrt(2.0 * math.pi)))).astype(BF)
        activ, slope = lax.optimization_barrier((activ, slope))

        down_grad = contract(activ, grad_low, 0, 0).astype(BF)
        late_line = lax.psum_scatter(
            down_grad.reshape(lines, 2, 2, block, width), "dev", scatter_dimension=0, axis_index_groups=groups
        )
        w_down = after(w_down, down_grad)
        pre_grad = (contract(grad_low, w_down, 1, 1) * slope.astype(F32)).astype(BF)
        mid_part = contract(pre_grad, w_up, 1, 1).astype(BF)
        mid_other = swap_core(mid_part)
        up_grad = contract(after(mid_low, mid_part), pre_grad, 0, 0).astype(BF)
        up_pick = parts_of(up_grad)
        up_give = give_far(up_pick)
        up_far = swap_a(up_give[0]), swap_b(up_give[1])
        up_b_grad = jnp.sum(pre_grad.astype(F32), axis=0)
        mid_other, _, _ = lax.optimization_barrier((mid_other, *up_give))
        mid_grad, attended_grad, proj_grad, *mid_sums = norm_back(
            core.reshape(1).astype(jnp.int32), mid, mid_part, mid_other, grad_low, gain_two, w_proj, attended
        )
        mid_grad, attended_grad, proj_grad, *up_far = lax.optimization_barrier(
            (mid_grad, attended_grad, proj_grad, *up_far)
        )
        gain_two_grad, shift_two_grad, proj_b_grad = (0.5 * item[0] for item in mid_sums)
        up_given = scatter_add(up_pick, up_far)
        up_near = scatter_near(up_given)
        proj_pick = parts_of(proj_grad)
        proj_give = give_far(proj_pick)
        proj_far = swap_a(proj_give[0]), swap_b(proj_give[1])
        proj_far = lax.optimization_barrier((*proj_far, *up_given))[:2]
        proj_given = scatter_add(proj_pick, proj_far)
        proj_near = scatter_near(proj_given)
        attended_grad = after(attended_grad, *proj_given, *up_given)
        qkv_back = attend_back(length, qkv, attended_grad, log_total).reshape(3 * side, rows)
        qkv_grad = contract(normed, qkv_back, 0, 1).astype(BF)
        qkv_grad, *up_near = lax.optimization_barrier((qkv_grad, *up_near))
        qkv_pick = parts_of(qkv_grad)
        qkv_give = give_far(qkv_pick)
        qkv_far = swap_a(qkv_give[0]), swap_b(qkv_give[1])
        normed_part = contract(after(qkv_back, *qkv_give), w_qkv[:, : 3 * side], 0, 1).astype(BF)
        normed_other = swap_core(rows_of(normed_part, other))
        came = lax.optimization_barrier((*up_near, *proj_near, normed_part))
        up_near, proj_near = came[:2], came[2:4]
        up_own = jnp.concatenate([scatter_own(up_pick, up_near), scatter_own(proj_pick, proj_near)], axis=2)
        up_sum = scatter_line(up_own)
        normed_part, late_line, up_own, *qkv_far = lax.optimization_barrier((normed_part, late_line, up_own, *qkv_far))
        qkv_given = scatter_add(qkv_pick, qkv_far)
        qkv_near = scatter_near(qkv_given)
        down_part = product(after(activ, *qkv_given), w_down)
        qkv_b_grad = jnp.sum(after(qkv_back, *qkv_given).astype(F32), axis=1)
        normed_part, *_ = lax.optimization_barrier((normed_part, *qkv_given))
        input_grad, gain_one_grad, shift_one_grad = first_back(
            core.reshape(1).astype(jnp.int32), tokens, normed_part, normed_other, mid_grad, gain_one
        )
        gain_one_grad, shift_one_grad = gain_one_grad[0], shift_one_grad[0]

        def on_side(vector):
            return lax.dynamic_update_slice(jnp.zeros((width,), F32), vector, (core * side,))

        up_rows = up_b_grad.reshape(chips, 1, shard, spread)
        up_rows = lax.dynamic_update_slice(
            jnp.zeros((chips, 2, shard, spread), F32), up_rows, (0, core, 0, 0)
        ).reshape(width, spread)
        sums = jnp.stack(
            [
                gain_one_grad,
                shift_one_grad,
                on_side(qkv_b_grad[:side]),
                on_side(qkv_b_grad[2 * side :]),
                proj_b_grad,
                gain_two_grad,
                shift_two_grad,
                down_b_grad,
            ],
            axis=1,
        )
        sums = jnp.concatenate([sums, up_rows], axis=1)
        sums = jnp.pad(sums, ((0, 0), (0, VECTORS - sums.shape[1]))).astype(BF)
        sums = after(sums, input_grad)
        sums = sums.reshape(lines, 2, 2, 2 * shard, VECTORS)

        def pick(b, a):
            at = lax.dynamic_index_in_dim(sums, b, 1, keepdims=False)
            return lax.dynamic_index_in_dim(at, a, 1, keepdims=False)

        def halves(parts, axis, at):
            own = lax.dynamic_index_in_dim(parts, at, axis, keepdims=False)
            return own, lax.dynamic_index_in_dim(parts, 1 - at, axis, keepdims=False)

        vector_come = swap_a(jnp.stack([pick(at_b, 1 - at_a), pick(1 - at_b, 1 - at_a)]))
        down_other = swap_core(rows_of(down_part, other))
        output = (
            rows_of(mid, core) + rows_of(down_part, core).astype(F32) + down_other.astype(F32) + b_down
        ).astype(BF)
        output, sums, vector_come, late_line, *qkv_near = lax.optimization_barrier(
            (output, sums, vector_come, late_line, *qkv_near)
        )
        vector_near = swap_b(pick(1 - at_b, at_a) + vector_come[1])
        late_keep, late_give = halves(late_line, 1, at_a)
        late_come = swap_a(late_give)
        qkv_own = scatter_own(qkv_pick, qkv_near)
        vector_own = pick(at_b, at_a) + vector_come[0] + vector_near
        own = jnp.concatenate([qkv_own, vector_own], axis=2)
        qkv_sum = scatter_line(own)
        late_keep, late_come, _ = lax.optimization_barrier((late_keep, late_come, own))
        late_keep, late_give = halves(late_keep + late_come, 0, at_b)
        late_sum = late_keep + swap_b(late_give)

        def finish(sum_of, which):
            return lax.dynamic_slice(sum_of, (which * shard, 0), (shard, sum_of.shape[1]))

        rest_mine = finish(up_sum, core)
        rest_theirs = swap_core(finish(up_sum, other))
        hidden_own = chips * block
        up_all = weave(core.reshape(1).astype(jnp.int32), rest_mine[:, :hidden_own], rest_theirs[:, :hidden_own], block)
        proj_mine, proj_theirs = rest_mine[:, hidden_own:], rest_theirs[:, hidden_own:]
        proj_all = jnp.concatenate(
            [jnp.where(core == 0, proj_mine, proj_theirs), jnp.where(core == 0, proj_theirs, proj_mine)], axis=1
        ).astype(F32)
        down_sum = late_sum
        qkv_sum = lax.optimization_barrier((qkv_sum, up_all, proj_all, down_sum, output))[0]
        query_all, key_all, value_all, vector_rows = unpack(
            core.reshape(1).astype(jnp.int32), qkv_sum, swap_core(qkv_sum), width
        )
        return (
            output,
            input_grad,
            vector_rows[:, 0],
            vector_rows[:, 1],
            query_all,
            vector_rows[:, 2],
            key_all,
            value_all,
            vector_rows[:, 3],
            proj_all,
            vector_rows[:, 4],
            vector_rows[:, 5],
            vector_rows[:, 6],
            up_all,
            vector_rows[:, 8 : 8 + spread].reshape(block),
            down_sum.astype(F32),
            vector_rows[:, 7],
        )

    return body


def solution(mesh):
    matrix, vector = P("dev", None), P("dev")
    return jax.shard_map(
        make_body(mesh.shape["dev"]),
        mesh=mesh,
        in_specs=(
            matrix,
            P(),
            matrix,
            vector,
            vector,
            matrix,
            vector,
            matrix,
            matrix,
            vector,
            matrix,
            vector,
            vector,
            vector,
            matrix,
            vector,
            matrix,
            vector,
        ),
        out_specs=(
            matrix,
            matrix,
            vector,
            vector,
            matrix,
            vector,
            matrix,
            matrix,
            vector,
            matrix,
            vector,
            vector,
            vector,
            matrix,
            vector,
            matrix,
            vector,
        ),
        check_vma=False,
    )
```
